256 devices in a mesh: grp: 4 (over y), dev: 64 (over x, z, core).
Axes of the slice: x: 4, y: 4, z: 8, core: 2. Of those that a mesh axis runs over, the one named last changes fastest.
Arguments:
- a_blocks: bfloat16 [32768, 4, 64, 64], P(('grp', 'dev')), may hold values from -6 to 6
- r_blocks: bfloat16 [32768, 64, 64], P(('grp', 'dev')), may hold values from -0.75 to 0.75
- p_blocks: bfloat16 [32768, 64, 64], P(('grp', 'dev')), may hold values from -0.75 to 0.75
- neighbours: int32 [32768, 3], P(('grp', 'dev')), may hold values from 0 to 319, as said below
- send_rows: int32 [256, 64, 3], P(('grp', 'dev')), may hold values from 0 to 127
- parent: int32 [32768], P(('grp', 'dev')), may hold values from 0 to 4095, as said below
- slot: int32 [32768, 4], P(('grp', 'dev')), may hold values from 0 to 6
Outputs:
- coarse_operator: float32 [4096, 7, 64, 64], P(('grp', 'dev'))
The draws below stay inside these ranges and needn't reach their ends.
Inputs may be any that keep to these rules, and one draw needn't show every extreme that they name: `neighbours`: with the notation of the steps: entries of device n below 128 are its own elements; every value from 128 to 319 appears exactly once among the entries of each device. The element at local position j of device n has its parent among the 16 coarse rows c * 16 to c * 16 + 15 of device c = (j // 32) * 64 + n % 64; each coarse row is the parent of an element in each of those blocks of 32 positions that point to it.
All inputs are finite; a program needn't handle non-finite values.
Results may differ from the reference program's by a relative error of at most 0.0029.
Values may be sent and summed in bfloat16 or wider, within the bound.
No kernel may reach another device: no remote copies, remote signals or barrier semaphores. Data moves between devices by JAX's collectives and lax.ppermute only.
A program may use at most 128 MiB of HBM per device.

```python
import jax
import jax.numpy as jnp
from jax import lax

B = 64
K = 3
S = 7
CAP = 3
E_DEV = 128
CR_DEV = 16
PEERS = 64
GROUPS = 4
NE = 32768
NC = 4096
NDEVS = 256
N_DEV = 64


def draw_neighbours(key, part):
    key = jax.random.fold_in(key, 7)
    received = PEERS * CAP

    def one_device(device_key):
        key_one, key_two = jax.random.split(device_key)
        entries = jax.random.randint(key_one, (E_DEV * K,), 0, E_DEV)
        places = jax.random.permutation(key_two, E_DEV * K)[:received]
        entries = entries.at[places].set(E_DEV + jnp.arange(received, dtype=jnp.int32))
        return entries.reshape(E_DEV, K)
    device_keys = jax.random.split(key, GROUPS * PEERS)
    return jax.vmap(one_device)(device_keys).reshape(NE, K).astype(jnp.int32)


def draw_parent(key, part):
    key = jax.random.fold_in(key, 13)
    group_span = E_DEV // GROUPS

    def one_block(block_key, device_index, block_index):
        key_one, key_two, key_three = jax.random.split(block_key, 3)
        covering = jax.random.permutation(key_one, CR_DEV)
        others = jax.random.randint(key_two, (group_span - CR_DEV,), 0, CR_DEV)
        coarse_rows = jax.random.permutation(key_three, jnp.concatenate([covering, others]))
        return (block_index * PEERS + device_index % PEERS) * CR_DEV + coarse_rows
    devices = jnp.repeat(jnp.arange(GROUPS * PEERS, dtype=jnp.int32), GROUPS)
    blocks = jnp.tile(jnp.arange(GROUPS, dtype=jnp.int32), GROUPS * PEERS)
    block_keys = jax.random.split(key, GROUPS * PEERS * GROUPS)
    return jax.vmap(one_block)(block_keys, devices, blocks).reshape(NE).astype(jnp.int32)


def set_ends(values, rng, least, high):
    extent = values.shape
    place = [jax.random.randint(jax.random.fold_in(rng, axis), (), 0, extent[axis]) for axis in range(len(extent))]
    values = values.at[tuple(place)].set(least)
    longest = extent.index(max(extent))
    place[longest] = (place[longest] + 1) % extent[longest]
    return values.at[tuple(place)].set(high)


def level_of(own_key, shape, cuts, low, high):
    def one(axis_at, shards_of):
        heights = jax.random.uniform(jax.random.fold_in(jax.random.fold_in(own_key, 6), axis_at), (shards_of,), jnp.float32, low / len(cuts), high / len(cuts))
        return jnp.repeat(jnp.exp(heights), shape[axis_at] // shards_of).reshape((-1,) + (1,) * (len(shape) - axis_at - 1))

    gain = one(*cuts[0])
    for cut in cuts[1:]:
        gain = gain * one(*cut)
    return gain


def scatter_about(rng, shape, deviation, bound, cuts=(), kind=jnp.bfloat16):
    array = deviation * jax.random.normal(rng, shape, jnp.float32)
    if cuts:
        array = array * level_of(rng, shape, cuts, -0.22, 0.18)
    return jnp.clip(array, -bound, bound).astype(kind)


def setup_inputs(seed: int = 0) -> dict:
    splits = jax.random.split(jax.random.key(seed), 8)
    return {
        "a_blocks": scatter_about(splits[0], (NE, K + 1, B, B), 1.0, 6.0, ((0, 256),)),
        "r_blocks": scatter_about(splits[1], (NE, B, B), B ** -0.5, 0.75, ((0, 256),)),
        "p_blocks": scatter_about(splits[2], (NE, B, B), B ** -0.5, 0.75, ((0, 256),)),
        "neighbours": draw_neighbours(jax.random.fold_in(splits[7], 71), 0),
        "send_rows": set_ends(jax.random.randint(splits[4], (NDEVS, N_DEV, CAP), 0, E_DEV), jax.random.fold_in(splits[4], 1), 0, E_DEV - 1).astype(jnp.int32),
        "parent": draw_parent(jax.random.fold_in(splits[7], 71), 0),
        "slot": set_ends(jax.random.randint(splits[6], (NE, K + 1), 0, S), jax.random.fold_in(splits[6], 1), 0, S - 1).astype(jnp.int32),
    }


def reference(a_blocks, r_blocks, p_blocks, neighbours, send_rows, parent, slot):
    def one_device(accumulated, device):
        group_index = device // N_DEV
        member = device % N_DEV
        start = (device * E_DEV).astype(jnp.int32)
        codes = lax.dynamic_slice_in_dim(neighbours, start, E_DEV, 0)
        offset = jnp.maximum(codes - E_DEV, 0)
        peer_index = group_index * N_DEV + offset // CAP
        sent_slot = offset % CAP
        remote_local = send_rows[peer_index, member, sent_slot]
        global_index = jnp.where(codes < E_DEV, start + codes, peer_index * E_DEV + remote_local).astype(jnp.int32)
        upwind = jnp.take(p_blocks, global_index, axis=0)
        own_blocks = lax.dynamic_slice_in_dim(p_blocks, start, E_DEV, 0)
        gathered = jnp.concatenate([own_blocks[:, None], upwind], 1).astype(jnp.float32)
        operator_rows = lax.dynamic_slice_in_dim(a_blocks, start, E_DEV, 0).astype(jnp.float32)
        applied = jnp.einsum("ekab,ekbc->ekac", operator_rows, gathered).astype(jnp.bfloat16)
        restrict = lax.dynamic_slice_in_dim(r_blocks, start, E_DEV, 0).astype(jnp.float32)
        products = jnp.einsum("eab,ekbc->ekac", restrict, applied.astype(jnp.float32)).reshape(E_DEV * (K + 1), B, B)
        parents = lax.dynamic_slice_in_dim(parent, start, E_DEV, 0)
        slots = lax.dynamic_slice_in_dim(slot, start, E_DEV, 0)
        segment_ids = (parents[:, None] * S + slots).reshape(-1).astype(jnp.int32)
        accumulated = accumulated.at[segment_ids].add(products)
        return accumulated, None

    initial = jnp.zeros((NC * S, B, B), jnp.float32)
    result, unused = lax.scan(one_device, initial, jnp.arange(NDEVS, dtype=jnp.int32))
    return result.reshape(NC, S, B, B)
```

```python
import functools

import jax
import jax.numpy as jnp
from jax import lax
from jax.experimental import pallas as pl
from jax.experimental.pallas import tpu as pltpu
from jax.sharding import PartitionSpec as P

MB = 1 << 20
F32 = jnp.float32
BF16 = jnp.bfloat16
VM = pltpu.VMEM
SM = pltpu.SMEM

E = 128
SPAN = 32
ROWS = 16
SLOTS = 7
BLOCKS = ROWS * SLOTS
HALF = BLOCKS // 2
FAR = 192
NEAR = 4 * E - FAR
CAP = 3 * SPAN
GROUP = 32
AREA = CAP + GROUP


def rows_at(index, size):
    return pl.ds(pl.multiple_of(index * size, size), size)


def transpose_slabs(slab_of, steps, stride, wide):
    @pl.loop(0, steps, unroll=8)
    def _(i):
        wide[pl.ds(i, E, stride=stride), :] = slab_of(i).astype(F32).T


def send_kernel(rows, p_ref, out_ref, packed, wide):
    transpose_slabs(
        lambda i: jnp.concatenate([p_ref[rows_at(i, 64), :], p_ref[rows_at(i + 32, 64), :]], 0), 32, 40, wide
    )
    packed[...] = wide[...].reshape(E, 40, 128)[:, :32].astype(BF16)

    @pl.loop(0, 64, unroll=4)
    def _(peer):
        for s in range(3):
            out_ref[peer * 3 + s] = packed[rows[s, peer]]


def send_blocks(rows, p_t):
    return pl.pallas_call(
        send_kernel,
        out_shape=jax.ShapeDtypeStruct((FAR, 32, 128), BF16),
        in_specs=[pl.BlockSpec(memory_space=SM), pl.BlockSpec(memory_space=VM)],
        out_specs=pl.BlockSpec(memory_space=VM),
        scratch_shapes=[VM((E, 32, 128), BF16), VM((E * 40, 128), F32)],
        compiler_params=pltpu.CompilerParams(vmem_limit_bytes=16 * MB),
        name="send_blocks",
    )(rows, p_t)


def term_of(pair, doubled):
    applied = jnp.dot(pair[:, :64], doubled, preferred_element_type=F32).astype(BF16)
    term = jnp.dot(pair[:, 64:], applied, preferred_element_type=F32)
    low = lax.broadcasted_iota(jnp.int32, (32, 128), 1) < 64
    return jnp.where(low, term[:32], term[32:])


def near_kernel(
    neighbours, slot, parent, a_ref, r_ref, p_ref,
    far_pairs, sums, counts, far_blocks, far_sums,
    pairs, doubled, wide, near_pairs, near_blocks, near_sums, far_list,
):
    def two(i):
        block = p_ref[rows_at(i, 64), :]
        return jnp.concatenate([block, block], 0)

    transpose_slabs(two, 64, 72, wide)
    doubled[...] = wide[...].reshape(E, 72, 128)[:, :64].astype(BF16)

    @pl.loop(0, 4)
    def _(k):
        transpose_slabs(
            lambda i: jnp.concatenate([a_ref[rows_at(k * 64 + i, 64), :], r_ref[rows_at(i, 64), :]], 0), 64, 72, wide
        )
        pairs[rows_at(k, E)] = wide[...].reshape(E, 72, 128)[:, :64].astype(BF16)

    sums[...] = jnp.zeros_like(sums)

    near = 0
    for j in range(4):
        start = j * AREA

        def element(i, carry):
            near, far = carry
            e = j * SPAN + i
            base = (parent[0, e] % ROWS) * SLOTS
            near_pairs[near] = e
            near_blocks[near] = e
            near_sums[near] = j * BLOCKS + base + slot[0, e]
            near = near + 1
            for k in range(1, 4):
                code = neighbours[k - 1, e]
                block_sum = base + slot[k, e]
                near_pairs[near] = k * E + e
                near_blocks[near] = code
                near_sums[near] = j * BLOCKS + block_sum
                far_list[far] = k * E + e
                far_blocks[far] = code - E
                far_sums[far] = block_sum
                here = (code < E).astype(jnp.int32)
                near = near + here
                far = far + (1 - here)
            return near, far

        near, far = lax.fori_loop(0, SPAN, element, (near, start))
        many = far - start
        counts[j] = many

        def keep(i, carry):
            far_pairs[j, i] = pairs[far_list[start + i]]
            return carry

        lax.fori_loop(0, many, keep, 0)

        def pad(i, carry):
            far_pairs[j, i] = jnp.zeros((64, 128), BF16)
            far_blocks[start + i] = 0
            far_sums[start + i] = 0
            return carry

        lax.fori_loop(many, (many + GROUP - 1) // GROUP * GROUP, pad, 0)

    @pl.loop(0, NEAR // GROUP)
    def _(g):
        found = [
            term_of(pairs[near_pairs[g * GROUP + u]], doubled[near_blocks[g * GROUP + u]]) for u in range(GROUP)
        ]
        for u in range(GROUP):
            sums[near_sums[g * GROUP + u]] += found[u]


def near_terms(neighbours, slot, parent, a_t, r_t, p_t):
    return pl.pallas_call(
        near_kernel,
        out_shape=[
            jax.ShapeDtypeStruct((4, CAP, 64, 128), BF16),
            jax.ShapeDtypeStruct((4 * BLOCKS, 32, 128), F32),
            jax.ShapeDtypeStruct((4,), jnp.int32),
            jax.ShapeDtypeStruct((4 * AREA,), jnp.int32),
            jax.ShapeDtypeStruct((4 * AREA,), jnp.int32),
        ],
        in_specs=[pl.BlockSpec(memory_space=SM)] * 3 + [pl.BlockSpec(memory_space=VM)] * 3,
        out_specs=[pl.BlockSpec(memory_space=VM)] * 2 + [pl.BlockSpec(memory_space=SM)] * 3,
        scratch_shapes=[
            VM((4 * E, 64, 128), BF16),
            VM((E, 64, 128), BF16),
            VM((E * 72, 128), F32),
            SM((NEAR + 8,), jnp.int32),
            SM((NEAR + 8,), jnp.int32),
            SM((NEAR + 8,), jnp.int32),
            SM((4 * AREA,), jnp.int32),
        ],
        compiler_params=pltpu.CompilerParams(vmem_limit_bytes=48 * MB),
        cost_estimate=pl.CostEstimate(flops=700_000_000, bytes_accessed=40_000_000, transcendentals=0),
        name="near_terms",
    )(neighbours, slot, parent, a_t, r_t, p_t)


def far_kernel(kinds, target, counts, far_blocks, far_sums, incoming, pairs, near, *refs):
    outs = refs[:-1]
    sums = refs[-1]
    sums[...] = near[0]
    j = target[0]
    start = j * AREA
    low = lax.broadcasted_iota(jnp.int32, (32, 128), 1) < 64

    def doubled(block):
        x = incoming[block]
        turned = jnp.concatenate([x[:, 64:], x[:, :64]], 1)
        return jnp.concatenate([jnp.where(low, x, turned), jnp.where(low, turned, x)], 0)

    def group(g, carry):
        at = g * GROUP
        found = [term_of(pairs[0, at + u], doubled(far_blocks[start + at + u])) for u in range(GROUP)]
        for u in range(GROUP):
            sums[far_sums[start + at + u]] += found[u]
        return carry

    lax.fori_loop(0, (counts[j] + GROUP - 1) // GROUP, group, 0)
    size = BLOCKS // len(kinds)
    for h, kind in enumerate(kinds):
        outs[h][...] = sums[h * size : (h + 1) * size].astype(kind)


def far_terms(kinds, target, lists, incoming, pairs, near, name):
    size = BLOCKS // len(kinds)
    return pl.pallas_call(
        functools.partial(far_kernel, kinds),
        grid_spec=pltpu.PrefetchScalarGridSpec(
            num_scalar_prefetch=4,
            grid=(1,),
            in_specs=[
                pl.BlockSpec((FAR, 32, 128), lambda i, target, *_: (0, 0, 0)),
                pl.BlockSpec((1, CAP, 64, 128), lambda i, target, *_: (target[0], 0, 0, 0)),
                pl.BlockSpec((1, BLOCKS, 32, 128), lambda i, target, *_: (target[0], 0, 0, 0)),
            ],
            out_specs=[pl.BlockSpec((size, 32, 128), lambda i, target, *_: (0, 0, 0))] * len(kinds),
            scratch_shapes=[VM((BLOCKS, 32, 128), F32)],
        ),
        out_shape=[jax.ShapeDtypeStruct((size, 32, 128), kind) for kind in kinds],
        compiler_params=pltpu.CompilerParams(vmem_limit_bytes=20 * MB),
        cost_estimate=pl.CostEstimate(flops=100_000_000, bytes_accessed=6_000_000, transcendentals=0),
        name=name,
    )(target, *lists, incoming, pairs, near)


def finish_kernel(own, low_a, low_b, high_a, high_b, out_ref):
    for h, (one, other) in enumerate(((low_a, low_b), (high_a, high_b))):
        total = own[h * HALF : (h + 1) * HALF] + one[...].astype(F32) + other[...].astype(F32)
        out_ref[h * HALF : (h + 1) * HALF, :32] = total[:, :, :64]
        out_ref[h * HALF : (h + 1) * HALF, 32:] = total[:, :, 64:]


def finish(*parts):
    return pl.pallas_call(
        finish_kernel,
        out_shape=jax.ShapeDtypeStruct((BLOCKS, 64, 64), F32),
        in_specs=[pl.BlockSpec(memory_space=VM)] * 5,
        out_specs=pl.BlockSpec(memory_space=VM),
        compiler_params=pltpu.CompilerParams(vmem_limit_bytes=24 * MB),
        name="finish",
    )(*parts)


def on_device(a_blocks, r_blocks, p_blocks, neighbours, send_rows, parent, slot):
    a_t = jnp.transpose(a_blocks, (1, 2, 3, 0)).reshape(4 * 4096, E)
    r_t = jnp.transpose(r_blocks, (1, 2, 0)).reshape(4096, E)
    p_t = jnp.transpose(p_blocks, (1, 2, 0)).reshape(4096, E)
    with jax.named_scope("exchange"):
        outgoing = send_blocks(jnp.transpose(send_rows, (2, 0, 1)).reshape(3, 64), p_t)
        incoming = lax.all_to_all(outgoing.reshape(64, 96, 128), "dev", 0, 0, tiled=True).reshape(FAR, 32, 128)
    with jax.named_scope("near"):
        pairs, near, *lists = near_terms(neighbours.T, slot.T, parent.reshape(1, E), a_t, r_t, p_t)
        near = near.reshape(4, BLOCKS, 32, 128)

    me = lax.axis_index("grp")

    def sums_of(ahead, kinds, name):
        target = ((me + ahead) % 4).astype(jnp.int32).reshape(1)
        return far_terms(kinds, target, lists, incoming, pairs, near, name)

    def to_next(x):
        return lax.ppermute(x, "grp", [(i, (i + 1) % 4) for i in range(4)])

    def to_last(x):
        return lax.ppermute(x, "grp", [(i, (i + 3) % 4) for i in range(4)])

    with jax.named_scope("far"):
        far_low, far_high = sums_of(2, (BF16, BF16), "far_two")
        passed_low, passed_high = to_next(far_low), to_last(far_high)
        next_low, next_high = sums_of(1, (F32, BF16), "far_next")
        from_last_high = to_next(next_high)
        last_low, last_high = sums_of(3, (BF16, F32), "far_last")
        from_next_low = to_last(last_low)
        from_last_low = to_next((next_low + passed_low.astype(F32)).astype(BF16))
        from_next_high = to_last((last_high + passed_high.astype(F32)).astype(BF16))
        (own,) = sums_of(0, (F32,), "far_own")
    with jax.named_scope("finish"):
        coarse = finish(own, from_last_low, from_next_low, from_last_high, from_next_high)
    return coarse.reshape(ROWS, SLOTS, 64, 64)


def solution(mesh):
    return jax.shard_map(
        on_device,
        mesh=mesh,
        in_specs=(
            P(("grp", "dev"), None, None, None),
            P(("grp", "dev"), None, None),
            P(("grp", "dev"), None, None),
            P(("grp", "dev"), None),
            P(("grp", "dev"), None, None),
            P(("grp", "dev")),
            P(("grp", "dev"), None),
        ),
        out_specs=P(("grp", "dev"), None, None, None),
        check_vma=False,
    )
```

```python
import functools

import jax
import jax.numpy as jnp
from jax import lax
from jax.experimental import pallas as pl
from jax.experimental.pallas import tpu as pltpu
from jax.sharding import PartitionSpec as P

MB = 1 << 20
F32 = jnp.float32
BF16 = jnp.bfloat16
VM = pltpu.VMEM
SM = pltpu.SMEM
HBM = pltpu.HBM

E = 128
SPAN = 32
ROWS = 16
SLOTS = 7
BLOCKS = ROWS * SLOTS
HALF = BLOCKS // 2
FAR = 192
CAP = 3 * SPAN
GROUP = 32
GROUPS = CAP // GROUP
AREA = CAP + GROUP
SUMS = 4 * AREA
COUNTS = 8 * AREA
AHEAD = (2, 1, 3, 0)


def rows_at(index, size):
    return pl.ds(pl.multiple_of(index * size, size), size)


def transpose_slabs(slab_of, steps, stride, wide, first=0):
    @pl.loop(0, steps, unroll=8)
    def _(i):
        wide[pl.ds(first + i, E, stride=stride), :] = slab_of(i).astype(F32).T


def send_kernel(rows, p_ref, out_ref, rows_here, blocks, packed, wide, arrived):
    rows_copy = pltpu.make_async_copy(rows, rows_here, arrived.at[4])
    rows_copy.start()
    copies = [
        pltpu.make_async_copy(p_ref.at[:, pl.ds(c * 8, 8)], blocks.at[c], arrived.at[c]) for c in range(4)
    ]
    for copy in copies:
        copy.start()
    for c in range(4):
        copies[c].wait()
        transpose_slabs(lambda i: blocks[c, :, i].reshape(128, E), 8, 40, wide, c * 8)
    packed[...] = wide[...].reshape(E, 40, 128)[:, :32].astype(BF16)
    rows_copy.wait()

    @pl.loop(0, 64, unroll=4)
    def _(peer):
        for s in range(3):
            out_ref[peer * 3 + s] = packed[rows_here[s, 0, peer]]


def send_blocks(rows, p_t):
    return pl.pallas_call(
        send_kernel,
        out_shape=jax.ShapeDtypeStruct((FAR, 32, 128), BF16),
        in_specs=[pl.BlockSpec(memory_space=HBM)] * 2,
        out_specs=pl.BlockSpec(memory_space=VM),
        scratch_shapes=[
            SM((3, 1, 64), jnp.int32),
            VM((4, 2, 8, 64, E), BF16),
            VM((E, 32, 128), BF16),
            VM((E * 40, 128), F32),
            pltpu.SemaphoreType.DMA((5,)),
        ],
        compiler_params=pltpu.CompilerParams(vmem_limit_bytes=63 * MB),
        name="send_blocks",
    )(rows, p_t)


def term_of(pair, doubled):
    applied = jnp.dot(pair[:, :64], doubled, preferred_element_type=F32).astype(BF16)
    term = jnp.dot(pair[:, 64:], applied, preferred_element_type=F32)
    low = lax.broadcasted_iota(jnp.int32, (32, 128), 1) < 64
    return jnp.where(low, term[:32], term[32:])


def near_kernel(me, neighbours, slot, parent, a_ref, r_ref, p_ref, *refs):
    far_pairs_out, sums_out, plan, pairs, doubled, wide, far_pairs, sums = refs[:8]
    near_pairs, near_blocks, near_sums, far_list, written = refs[8:]
    copies = []

    def two(i):
        block = p_ref[rows_at(i, 64), :]
        return jnp.concatenate([block, block], 0)

    transpose_slabs(two, 64, 72, wide)
    doubled[...] = wide[...].reshape(E, 72, 128)[:, :64].astype(BF16)

    @pl.loop(0, 4)
    def _(k):
        transpose_slabs(
            lambda i: jnp.concatenate([a_ref[rows_at(k * 64 + i, 64), :], r_ref[rows_at(i, 64), :]], 0), 64, 72, wide
        )
        pairs[rows_at(k, E)] = wide[...].reshape(E, 72, 128)[:, :64].astype(BF16)

    pairs[4 * E] = jnp.zeros((64, 128), BF16)

    for part, ahead in enumerate(AHEAD):
        first = lax.rem(me[0] + ahead, 4) * SPAN
        start = part * AREA

        def element(i, carry):
            near, far = carry
            e = first + i
            base = lax.rem(parent[0, e], ROWS) * SLOTS
            near_pairs[near] = e
            near_blocks[near] = e
            near_sums[near] = base + slot[0, e]
            near = near + 1
            for k in range(1, 4):
                code = neighbours[k - 1, e]
                block_sum = base + slot[k, e]
                near_pairs[near] = k * E + e
                near_blocks[near] = code
                near_sums[near] = block_sum
                far_list[far] = k * E + e
                plan[far] = code - E
                plan[SUMS + far] = block_sum
                here = (code < E).astype(jnp.int32)
                near = near + here
                far = far + (1 - here)
            return near, far

        near, far = lax.fori_loop(0, SPAN, element, (0, start))
        many = far - start
        plan[COUNTS + part] = many

        def keep(i, carry):
            far_pairs[part, i] = pairs[far_list[start + i]]
            return carry

        lax.fori_loop(0, many, keep, 0)

        def pad_far(i, carry):
            far_pairs[part, i] = jnp.zeros((64, 128), BF16)
            plan[start + i] = 0
            plan[SUMS + start + i] = 0
            return carry

        lax.fori_loop(many, (many + GROUP - 1) // GROUP * GROUP, pad_far, 0)

        def pad_near(i, carry):
            near_pairs[i] = 4 * E
            near_blocks[i] = 0
            near_sums[i] = 0
            return carry

        copies.append(pltpu.make_async_copy(far_pairs.at[part], far_pairs_out.at[part], written.at[part]))
        copies[-1].start()
        groups = (near + GROUP - 1) // GROUP
        lax.fori_loop(near, groups * GROUP, pad_near, 0)
        sums[part] = jnp.zeros((BLOCKS, 32, 128), F32)

        def group(g, carry):
            at = g * GROUP
            found = [term_of(pairs[near_pairs[at + u]], doubled[near_blocks[at + u]]) for u in range(GROUP)]
            for u in range(GROUP):
                sums[part, near_sums[at + u]] += found[u]
            return carry

        lax.fori_loop(0, groups, group, 0)
        copies.append(pltpu.make_async_copy(sums.at[part], sums_out.at[part], written.at[4 + part]))
        copies[-1].start()

    for copy in copies:
        copy.wait()


def near_terms(me, neighbours, slot, parent, a_t, r_t, p_t):
    return pl.pallas_call(
        near_kernel,
        out_shape=[
            jax.ShapeDtypeStruct((4, CAP, 64, 128), BF16),
            jax.ShapeDtypeStruct((4, BLOCKS, 32, 128), F32),
        ]
        + [jax.ShapeDtypeStruct((COUNTS + 8,), jnp.int32)],
        in_specs=[pl.BlockSpec(memory_space=SM)] * 4 + [pl.BlockSpec(memory_space=VM)] * 3,
        out_specs=[pl.BlockSpec(memory_space=HBM)] * 2 + [pl.BlockSpec(memory_space=SM)],
        scratch_shapes=[
            VM((4 * E + 1, 64, 128), BF16),
            VM((E, 64, 128), BF16),
            VM((E * 72, 128), F32),
            VM((4, CAP, 64, 128), BF16),
            VM((4, BLOCKS, 32, 128), F32),
            SM((4 * SPAN + GROUP,), jnp.int32),
            SM((4 * SPAN + GROUP,), jnp.int32),
            SM((4 * SPAN + GROUP,), jnp.int32),
            SM((4 * AREA,), jnp.int32),
            pltpu.SemaphoreType.DMA((8,)),
        ],
        compiler_params=pltpu.CompilerParams(vmem_limit_bytes=55 * MB),
        cost_estimate=pl.CostEstimate(flops=700_000_000, bytes_accessed=40_000_000, transcendentals=0),
        name="near_terms",
    )(me, neighbours, slot, parent, a_t, r_t, p_t)


def far_kernel(parts, kinds, plan, incoming, *refs):
    pairs_in, near_in, *outs = refs[:-4]
    pairs, near, sums, arrived = refs[-4:]
    low = lax.broadcasted_iota(jnp.int32, (32, 128), 1) < 64

    def pairs_copy(n, g):
        some = pl.ds(g * GROUP, GROUP)
        return pltpu.make_async_copy(pairs_in.at[parts[n], some], pairs.at[n, some], arrived.at[n, g])

    def near_copy(n):
        return pltpu.make_async_copy(near_in.at[parts[n]], near.at[n], arrived.at[n, GROUPS])

    def doubled(block):
        x = incoming[block]
        turned = jnp.concatenate([x[:, 64:], x[:, :64]], 1)
        return jnp.concatenate([jnp.where(low, x, turned), jnp.where(low, turned, x)], 0)

    for n, part in enumerate(parts):
        for g in range(GROUPS):

            @pl.when(plan[COUNTS + part] > g * GROUP)
            def _(n=n, g=g):
                pairs_copy(n, g).start()

        near_copy(n).start()

    for n, part in enumerate(parts):
        sums[...] = jnp.zeros_like(sums)
        start = part * AREA
        groups = (plan[COUNTS + part] + GROUP - 1) // GROUP

        def group(g, carry):
            at = g * GROUP
            pairs_copy(n, g).wait()
            found = [term_of(pairs[n, at + u], doubled(plan[start + at + u])) for u in range(GROUP)]
            for u in range(GROUP):
                sums[plan[SUMS + start + at + u]] += found[u]
            return carry

        lax.fori_loop(0, groups, group, 0)
        near_copy(n).wait()
        size = BLOCKS // len(kinds[n])
        for h, kind in enumerate(kinds[n]):
            some = pl.ds(h * size, size)
            outs[2 * n + h][...] = (near[n, some] + sums[some]).astype(kind)


def far_terms(parts, kinds, plan, incoming, pairs, near, name):
    shapes = [(BLOCKS // len(some), kind) for some in kinds for kind in some]
    return pl.pallas_call(
        functools.partial(far_kernel, parts, kinds),
        in_specs=[pl.BlockSpec(memory_space=SM), pl.BlockSpec(memory_space=VM)]
        + [pl.BlockSpec(memory_space=HBM)] * 2,
        out_specs=[pl.BlockSpec(memory_space=VM)] * len(shapes),
        scratch_shapes=[
            VM((len(parts), CAP, 64, 128), BF16),
            VM((len(parts), BLOCKS, 32, 128), F32),
            VM((BLOCKS, 32, 128), F32),
            pltpu.SemaphoreType.DMA((len(parts), GROUPS + 1)),
        ],
        out_shape=[jax.ShapeDtypeStruct((size, 32, 128), kind) for size, kind in shapes],
        compiler_params=pltpu.CompilerParams(vmem_limit_bytes=48 * MB),
        cost_estimate=pl.CostEstimate(flops=100_000_000, bytes_accessed=6_000_000, transcendentals=0),
        name=name,
    )(plan, incoming, pairs, near)


def add_kernel(here_a, passed_a, here_b, passed_b, out_a, out_b):
    out_a[...] = (here_a[...] + passed_a[...].astype(F32)).astype(BF16)
    out_b[...] = (here_b[...] + passed_b[...].astype(F32)).astype(BF16)


def add_passed(*parts):
    return pl.pallas_call(
        add_kernel,
        out_shape=[jax.ShapeDtypeStruct((HALF, 32, 128), BF16)] * 2,
        in_specs=[pl.BlockSpec(memory_space=VM)] * 4,
        out_specs=[pl.BlockSpec(memory_space=VM)] * 2,
        compiler_params=pltpu.CompilerParams(vmem_limit_bytes=16 * MB),
        name="add_passed",
    )(*parts)


def finish_kernel(own, low_a, low_b, high_a, high_b, out_ref):
    for h, (one, other) in enumerate(((low_a, low_b), (high_a, high_b))):
        total = own[h * HALF : (h + 1) * HALF] + one[...].astype(F32) + other[...].astype(F32)
        out_ref[h * HALF : (h + 1) * HALF, :32] = total[:, :, :64]
        out_ref[h * HALF : (h + 1) * HALF, 32:] = total[:, :, 64:]


def finish(*parts):
    return pl.pallas_call(
        finish_kernel,
        out_shape=jax.ShapeDtypeStruct((BLOCKS, 64, 64), F32),
        in_specs=[pl.BlockSpec(memory_space=VM)] * 5,
        out_specs=pl.BlockSpec(memory_space=VM),
        compiler_params=pltpu.CompilerParams(vmem_limit_bytes=24 * MB),
        name="finish",
    )(*parts)


def on_device(a_blocks, r_blocks, p_blocks, neighbours, send_rows, parent, slot):
    a_t = jnp.transpose(a_blocks, (1, 2, 3, 0)).reshape(4 * 4096, E)
    r_t = jnp.transpose(r_blocks, (1, 2, 0)).reshape(4096, E)
    p_t = jnp.transpose(p_blocks, (1, 2, 0))
    me = lax.axis_index("grp").astype(jnp.int32).reshape(1)
    with jax.named_scope("exchange"):
        outgoing = send_blocks(jnp.transpose(send_rows, (2, 0, 1)), p_t.reshape(2, 32, 64, E))
        incoming = lax.all_to_all(outgoing.reshape(64, 96, 128), "dev", 0, 0, tiled=True).reshape(FAR, 32, 128)
    with jax.named_scope("near"):
        pairs, near, plan = near_terms(
            me, neighbours.T, slot.T, parent.reshape(1, E), a_t, r_t, p_t.reshape(4096, E)
        )

    def to_next(x):
        return lax.ppermute(x, "grp", [(i, (i + 1) % 4) for i in range(4)])

    def to_last(x):
        return lax.ppermute(x, "grp", [(i, (i + 3) % 4) for i in range(4)])

    with jax.named_scope("far"):
        far_low, far_high = far_terms((0,), ((BF16, BF16),), plan, incoming, pairs, near, "far_two")
        passed_low, passed_high = to_next(far_low), to_last(far_high)
        next_low, next_high, last_low, last_high = far_terms(
            (1, 2), ((F32, BF16), (BF16, F32)), plan, incoming, pairs, near, "far_one"
        )
        from_last_high, from_next_low = to_next(next_high), to_last(last_low)
        both_low, both_high = add_passed(next_low, passed_low, last_high, passed_high)
        from_last_low, from_next_high = to_next(both_low), to_last(both_high)
        (own,) = far_terms((3,), ((F32,),), plan, incoming, pairs, near, "far_own")
    with jax.named_scope("finish"):
        coarse = finish(own, from_last_low, from_next_low, from_last_high, from_next_high)
    return coarse.reshape(ROWS, SLOTS, 64, 64)


def solution(mesh):
    return jax.shard_map(
        on_device,
        mesh=mesh,
        in_specs=(
            P(("grp", "dev"), None, None, None),
            P(("grp", "dev"), None, None),
            P(("grp", "dev"), None, None),
            P(("grp", "dev"), None),
            P(("grp", "dev"), None, None),
            P(("grp", "dev")),
            P(("grp", "dev"), None),
        ),
        out_specs=P(("grp", "dev"), None, None, None),
        check_vma=False,
    )
```

```python
import functools

import jax
import jax.numpy as jnp
from jax import lax
from jax.experimental import pallas as pl
from jax.experimental.pallas import tpu as pltpu
from jax.sharding import PartitionSpec as P

MB = 1 << 20
F32 = jnp.float32
BF16 = jnp.bfloat16
VM = pltpu.VMEM
SM = pltpu.SMEM
HBM = pltpu.HBM

E = 128
SPAN = 32
ROWS = 16
SLOTS = 7
BLOCKS = ROWS * SLOTS
HALF = BLOCKS // 2
FAR = 192
CAP = 3 * SPAN
GROUP = 32
GROUPS = CAP // GROUP
CHUNKS = 4
AREA = CAP + GROUP
SUMS = 4 * AREA
COUNTS = 8 * AREA
PLAN = COUNTS + 1024
ROOM = 3 * MB
AHEAD = (2, 1, 3, 0)


def rows_at(index, size):
    return pl.ds(pl.multiple_of(index * size, size), size)


def transpose_slabs(slab_of, steps, stride, wide, first=0):
    @pl.loop(0, steps, unroll=8)
    def _(i):
        wide[pl.ds(first + i, E, stride=stride), :] = slab_of(i).astype(F32).T


def send_kernel(rows, p_ref, out_ref, rows_here, blocks, packed, wide, outgoing, arrived, written):
    rows_copy = pltpu.make_async_copy(rows, rows_here, arrived.at[4])
    rows_copy.start()
    copies = [
        pltpu.make_async_copy(p_ref.at[:, pl.ds(c * 8, 8)], blocks.at[c], arrived.at[c]) for c in range(4)
    ]
    for copy in copies:
        copy.start()
    for c in range(4):
        copies[c].wait()
        transpose_slabs(lambda i: blocks[c, :, i].reshape(128, E), 8, 40, wide, c * 8)
    packed[...] = wide[...].reshape(E, 40, 128)[:, :32].astype(BF16)
    rows_copy.wait()

    copies = []
    for c in range(CHUNKS):
        size = FAR // CHUNKS

        @pl.loop(0, 64 // CHUNKS, unroll=4)
        def _(n):
            peer = c * (64 // CHUNKS) + n
            for s in range(3):
                outgoing[peer * 3 + s] = packed[rows_here[s, 0, peer]]

        some = pl.ds(c * size, size)
        copies.append(pltpu.make_async_copy(outgoing.at[some], out_ref.at[some], written.at[c]))
        copies[-1].start()
    for copy in copies:
        copy.wait()


def send_blocks(rows, p_t):
    return pl.pallas_call(
        send_kernel,
        out_shape=jax.ShapeDtypeStruct((FAR, 32, 128), BF16),
        in_specs=[pl.BlockSpec(memory_space=HBM)] * 2,
        out_specs=pl.BlockSpec(memory_space=HBM),
        scratch_shapes=[
            SM((3, 1, 64), jnp.int32),
            VM((4, 2, 8, 64, E), BF16),
            VM((E, 32, 128), BF16),
            VM((E * 40, 128), F32),
            VM((FAR, 32, 128), BF16),
            pltpu.SemaphoreType.DMA((5,)),
            pltpu.SemaphoreType.DMA((CHUNKS,)),
        ],
        compiler_params=pltpu.CompilerParams(vmem_limit_bytes=63 * MB),
        name="send_blocks",
    )(rows, p_t)


def term_of(pair, doubled):
    applied = jnp.dot(pair[:, :64], doubled, preferred_element_type=F32).astype(BF16)
    term = jnp.dot(pair[:, 64:], applied, preferred_element_type=F32)
    low = lax.broadcasted_iota(jnp.int32, (32, 128), 1) < 64
    return jnp.where(low, term[:32], term[32:])


def near_kernel(me, neighbours, slot, parent, a_ref, r_ref, p_ref, *refs):
    far_pairs_out, sums_out, plan_out, pairs, doubled, wide, far_pairs, sums = refs[:8]
    plan, near_pairs, near_blocks, near_sums, far_list, written = refs[8:]
    copies = []

    def two(i):
        block = p_ref[rows_at(i, 64), :]
        return jnp.concatenate([block, block], 0)

    transpose_slabs(two, 64, 72, wide)
    doubled[...] = wide[...].reshape(E, 72, 128)[:, :64].astype(BF16)

    @pl.loop(0, 4)
    def _(k):
        transpose_slabs(
            lambda i: jnp.concatenate([a_ref[rows_at(k * 64 + i, 64), :], r_ref[rows_at(i, 64), :]], 0), 64, 72, wide
        )
        pairs[rows_at(k, E)] = wide[...].reshape(E, 72, 128)[:, :64].astype(BF16)

    pairs[4 * E] = jnp.zeros((64, 128), BF16)

    for part, ahead in enumerate(AHEAD):
        first = lax.rem(me[0] + ahead, 4) * SPAN
        start = part * AREA

        def element(i, carry):
            near, far = carry
            e = first + i
            base = lax.rem(parent[0, e], ROWS) * SLOTS
            near_pairs[near] = e
            near_blocks[near] = e
            near_sums[near] = base + slot[0, e]
            near = near + 1
            for k in range(1, 4):
                code = neighbours[k - 1, e]
                block_sum = base + slot[k, e]
                near_pairs[near] = k * E + e
                near_blocks[near] = code
                near_sums[near] = block_sum
                far_list[far] = k * E + e
                plan[far] = code - E
                plan[SUMS + far] = block_sum
                here = (code < E).astype(jnp.int32)
                near = near + here
                far = far + (1 - here)
            return near, far

        near, far = lax.fori_loop(0, SPAN, element, (0, start))
        many = far - start
        plan[COUNTS + part] = many

        def keep(i, carry):
            far_pairs[part, i] = pairs[far_list[start + i]]
            return carry

        lax.fori_loop(0, many, keep, 0)

        def pad_far(i, carry):
            far_pairs[part, i] = jnp.zeros((64, 128), BF16)
            plan[start + i] = 0
            plan[SUMS + start + i] = 0
            return carry

        lax.fori_loop(many, (many + GROUP - 1) // GROUP * GROUP, pad_far, 0)

        def pad_near(i, carry):
            near_pairs[i] = 4 * E
            near_blocks[i] = 0
            near_sums[i] = 0
            return carry

        copies.append(pltpu.make_async_copy(far_pairs.at[part], far_pairs_out.at[part], written.at[part]))
        copies[-1].start()
        groups = (near + GROUP - 1) // GROUP
        lax.fori_loop(near, groups * GROUP, pad_near, 0)
        sums[part] = jnp.zeros((BLOCKS, 32, 128), F32)

        def group(g, carry):
            at = g * GROUP
            found = [term_of(pairs[near_pairs[at + u]], doubled[near_blocks[at + u]]) for u in range(GROUP)]
            for u in range(GROUP):
                sums[part, near_sums[at + u]] += found[u]
            return carry

        lax.fori_loop(0, groups, group, 0)
        copies.append(pltpu.make_async_copy(sums.at[part], sums_out.at[part], written.at[4 + part]))
        copies[-1].start()

    copies.append(pltpu.make_async_copy(plan, plan_out.at[pl.ds(0, PLAN)], written.at[8]))
    copies[-1].start()
    for copy in copies:
        copy.wait()


def near_terms(me, neighbours, slot, parent, a_t, r_t, p_t):
    return pl.pallas_call(
        near_kernel,
        out_shape=[
            jax.ShapeDtypeStruct((4, CAP, 64, 128), BF16),
            jax.ShapeDtypeStruct((4, BLOCKS, 32, 128), F32),
        ]
        + [jax.ShapeDtypeStruct((ROOM,), jnp.int32)],
        in_specs=[pl.BlockSpec(memory_space=SM)] * 4 + [pl.BlockSpec(memory_space=VM)] * 3,
        out_specs=[pl.BlockSpec(memory_space=HBM)] * 3,
        scratch_shapes=[
            VM((4 * E + 1, 64, 128), BF16),
            VM((E, 64, 128), BF16),
            VM((E * 72, 128), F32),
            VM((4, CAP, 64, 128), BF16),
            VM((4, BLOCKS, 32, 128), F32),
            SM((PLAN,), jnp.int32),
            SM((4 * SPAN + GROUP,), jnp.int32),
            SM((4 * SPAN + GROUP,), jnp.int32),
            SM((4 * SPAN + GROUP,), jnp.int32),
            SM((4 * AREA,), jnp.int32),
            pltpu.SemaphoreType.DMA((9,)),
        ],
        compiler_params=pltpu.CompilerParams(vmem_limit_bytes=55 * MB),
        cost_estimate=pl.CostEstimate(flops=700_000_000, bytes_accessed=40_000_000, transcendentals=0),
        name="near_terms",
    )(me, neighbours, slot, parent, a_t, r_t, p_t)


def far_kernel(parts, kinds, plan_in, incoming, *refs):
    pairs_in, near_in, *outs = refs[:-6]
    plan, pairs, near, sums, arrived, plan_arrived = refs[-6:]
    plan_copy = pltpu.make_async_copy(plan_in.at[pl.ds(0, PLAN)], plan, plan_arrived)
    plan_copy.start()
    low = lax.broadcasted_iota(jnp.int32, (32, 128), 1) < 64

    def pairs_copy(n, g):
        some = pl.ds(g * GROUP, GROUP)
        return pltpu.make_async_copy(pairs_in.at[parts[n], some], pairs.at[n, some], arrived.at[n, g])

    def near_copy(n):
        return pltpu.make_async_copy(near_in.at[parts[n]], near.at[n], arrived.at[n, GROUPS])

    def doubled(block):
        x = incoming[block]
        turned = jnp.concatenate([x[:, 64:], x[:, :64]], 1)
        return jnp.concatenate([jnp.where(low, x, turned), jnp.where(low, turned, x)], 0)

    for n in range(len(parts)):
        pairs_copy(n, 0).start()
        near_copy(n).start()
    plan_copy.wait()
    for n, part in enumerate(parts):
        for g in range(1, GROUPS):

            @pl.when(plan[COUNTS + part] > g * GROUP)
            def _(n=n, g=g):
                pairs_copy(n, g).start()


    for n, part in enumerate(parts):
        sums[...] = jnp.zeros_like(sums)
        start = part * AREA
        groups = (plan[COUNTS + part] + GROUP - 1) // GROUP

        def group(g, carry):
            at = g * GROUP
            pairs_copy(n, g).wait()
            found = [term_of(pairs[n, at + u], doubled(plan[start + at + u])) for u in range(GROUP)]
            for u in range(GROUP):
                sums[plan[SUMS + start + at + u]] += found[u]
            return carry

        lax.fori_loop(0, groups, group, 0)

        @pl.when(groups == 0)
        def _(n=n):
            pairs_copy(n, 0).wait()

        near_copy(n).wait()
        size = BLOCKS // len(kinds[n])
        for h, kind in enumerate(kinds[n]):
            some = pl.ds(h * size, size)
            outs[2 * n + h][...] = (near[n, some] + sums[some]).astype(kind)


def far_terms(parts, kinds, plan, incoming, pairs, near, name):
    shapes = [(BLOCKS // len(some), kind) for some in kinds for kind in some]
    return pl.pallas_call(
        functools.partial(far_kernel, parts, kinds),
        in_specs=[pl.BlockSpec(memory_space=HBM), pl.BlockSpec(memory_space=VM)]
        + [pl.BlockSpec(memory_space=HBM)] * 2,
        out_specs=[pl.BlockSpec(memory_space=VM)] * len(shapes),
        scratch_shapes=[
            SM((PLAN,), jnp.int32),
            VM((len(parts), CAP, 64, 128), BF16),
            VM((len(parts), BLOCKS, 32, 128), F32),
            VM((BLOCKS, 32, 128), F32),
            pltpu.SemaphoreType.DMA((len(parts), GROUPS + 1)),
            pltpu.SemaphoreType.DMA,
        ],
        out_shape=[jax.ShapeDtypeStruct((size, 32, 128), kind) for size, kind in shapes],
        compiler_params=pltpu.CompilerParams(vmem_limit_bytes=48 * MB),
        cost_estimate=pl.CostEstimate(flops=100_000_000, bytes_accessed=6_000_000, transcendentals=0),
        name=name,
    )(plan, incoming, pairs, near)


def add_kernel(here_a, passed_a, here_b, passed_b, out_a, out_b):
    out_a[...] = (here_a[...] + passed_a[...].astype(F32)).astype(BF16)
    out_b[...] = (here_b[...] + passed_b[...].astype(F32)).astype(BF16)


def add_passed(*parts):
    return pl.pallas_call(
        add_kernel,
        out_shape=[jax.ShapeDtypeStruct((HALF, 32, 128), BF16)] * 2,
        in_specs=[pl.BlockSpec(memory_space=VM)] * 4,
        out_specs=[pl.BlockSpec(memory_space=VM)] * 2,
        compiler_params=pltpu.CompilerParams(vmem_limit_bytes=16 * MB),
        name="add_passed",
    )(*parts)


def finish_kernel(own, low_a, low_b, high_a, high_b, out_ref, totals, written):
    copies = []
    size = BLOCKS // CHUNKS
    for c in range(CHUNKS):
        one, other = ((low_a, low_b), (high_a, high_b))[c * 2 // CHUNKS]
        some = pl.ds(c * size, size)
        here = pl.ds(c * size % HALF, size)
        total = own[some] + one[here].astype(F32) + other[here].astype(F32)
        totals[some, :32] = total[:, :, :64]
        totals[some, 32:] = total[:, :, 64:]
        copies.append(pltpu.make_async_copy(totals.at[some], out_ref.at[some], written.at[c]))
        copies[-1].start()
    for copy in copies:
        copy.wait()


def finish(*parts):
    return pl.pallas_call(
        finish_kernel,
        out_shape=jax.ShapeDtypeStruct((BLOCKS, 64, 64), F32),
        in_specs=[pl.BlockSpec(memory_space=VM)] * 5,
        out_specs=pl.BlockSpec(memory_space=HBM),
        scratch_shapes=[VM((BLOCKS, 64, 64), F32), pltpu.SemaphoreType.DMA((CHUNKS,))],
        compiler_params=pltpu.CompilerParams(vmem_limit_bytes=24 * MB),
        name="finish",
    )(*parts)


def on_device(a_blocks, r_blocks, p_blocks, neighbours, send_rows, parent, slot):
    a_t = jnp.transpose(a_blocks, (1, 2, 3, 0)).reshape(4 * 4096, E)
    r_t = jnp.transpose(r_blocks, (1, 2, 0)).reshape(4096, E)
    p_t = jnp.transpose(p_blocks, (1, 2, 0))
    me = lax.axis_index("grp").astype(jnp.int32).reshape(1)
    with jax.named_scope("exchange"):
        outgoing = send_blocks(jnp.transpose(send_rows, (2, 0, 1)), p_t.reshape(2, 32, 64, E))
        incoming = lax.all_to_all(outgoing.reshape(64, 96, 128), "dev", 0, 0, tiled=True).reshape(FAR, 32, 128)
    with jax.named_scope("near"):
        pairs, near, plan = near_terms(
            me, neighbours.T, slot.T, parent.reshape(1, E), a_t, r_t, p_t.reshape(4096, E)
        )

    def to_next(x):
        return lax.ppermute(x, "grp", [(i, (i + 1) % 4) for i in range(4)])

    def to_last(x):
        return lax.ppermute(x, "grp", [(i, (i + 3) % 4) for i in range(4)])

    with jax.named_scope("far"):
        far_low, far_high = far_terms((0,), ((BF16, BF16),), plan, incoming, pairs, near, "far_two")
        passed_low, passed_high = to_next(far_low), to_last(far_high)
        next_low, next_high, last_low, last_high = far_terms(
            (1, 2), ((F32, BF16), (BF16, F32)), plan, incoming, pairs, near, "far_one"
        )
        from_last_high, from_next_low = to_next(next_high), to_last(last_low)
        both_low, both_high = add_passed(next_low, passed_low, last_high, passed_high)
        from_last_low, from_next_high = to_next(both_low), to_last(both_high)
        (own,) = far_terms((3,), ((F32,),), plan, incoming, pairs, near, "far_own")
    with jax.named_scope("finish"):
        coarse = finish(own, from_last_low, from_next_low, from_last_high, from_next_high)
    return coarse.reshape(ROWS, SLOTS, 64, 64)


def solution(mesh):
    return jax.shard_map(
        on_device,
        mesh=mesh,
        in_specs=(
            P(("grp", "dev"), None, None, None),
            P(("grp", "dev"), None, None),
            P(("grp", "dev"), None, None),
            P(("grp", "dev"), None),
            P(("grp", "dev"), None, None),
            P(("grp", "dev")),
            P(("grp", "dev"), None),
        ),
        out_specs=P(("grp", "dev"), None, None, None),
        check_vma=False,
    )
```

```python
import functools

import jax
import jax.numpy as jnp
from jax import lax
from jax.experimental import pallas as pl
from jax.experimental.pallas import tpu as pltpu
from jax.sharding import PartitionSpec as P

MB = 1 << 20
F32 = jnp.float32
BF16 = jnp.bfloat16
VM = pltpu.VMEM
SM = pltpu.SMEM
HBM = pltpu.HBM

E = 128
SPAN = 32
ROWS = 16
SLOTS = 7
BLOCKS = ROWS * SLOTS
HALF = BLOCKS // 2
FAR = 192
CAP = 3 * SPAN
GROUP = 32
GROUPS = CAP // GROUP
FIRST = 40
CHUNKS = 4
AREA = CAP + GROUP
SUMS = 4 * AREA
COUNTS = 8 * AREA
PLAN = COUNTS + 1024
ROOM = 3 * MB
AHEAD = (2, 1, 3, 0)


def rows_at(index, size):
    return pl.ds(pl.multiple_of(index * size, size), size)


def transpose_slabs(slab_of, steps, stride, wide, first=0):
    @pl.loop(0, steps, unroll=8)
    def _(i):
        wide[pl.ds(first + i, E, stride=stride), :] = slab_of(i).astype(F32).T


def send_kernel(rows, p_ref, out_ref, rows_here, blocks, wide, outgoing, arrived, written):
    rows_copy = pltpu.make_async_copy(rows, rows_here, arrived.at[4])
    rows_copy.start()
    copies = [
        pltpu.make_async_copy(p_ref.at[:, pl.ds(c * 8, 8)], blocks.at[c], arrived.at[c]) for c in range(4)
    ]
    for copy in copies:
        copy.start()
    for c in range(4):
        copies[c].wait()
        transpose_slabs(lambda i: blocks[c, :, i].reshape(128, E), 8, 40, wide, c * 8)
    rows_copy.wait()

    copies = []
    for c in range(CHUNKS):
        size = FAR // CHUNKS

        @pl.loop(0, 64 // CHUNKS, unroll=4)
        def _(n):
            peer = c * (64 // CHUNKS) + n
            for s in range(3):
                row = pl.multiple_of(rows_here[s, 0, peer] * 40, 8)
                outgoing[peer * 3 + s] = wide[pl.ds(row, 32), :].astype(BF16)

        some = pl.ds(c * size, size)
        copies.append(pltpu.make_async_copy(outgoing.at[some], out_ref.at[some], written.at[c]))
        copies[-1].start()
    for copy in copies:
        copy.wait()


def send_blocks(rows, p_t):
    return pl.pallas_call(
        send_kernel,
        out_shape=jax.ShapeDtypeStruct((FAR, 32, 128), BF16),
        in_specs=[pl.BlockSpec(memory_space=HBM)] * 2,
        out_specs=pl.BlockSpec(memory_space=HBM),
        scratch_shapes=[
            SM((3, 1, 64), jnp.int32),
            VM((4, 2, 8, 64, E), BF16),
            VM((E * 40, 128), F32),
            VM((FAR, 32, 128), BF16),
            pltpu.SemaphoreType.DMA((5,)),
            pltpu.SemaphoreType.DMA((CHUNKS,)),
        ],
        compiler_params=pltpu.CompilerParams(vmem_limit_bytes=63 * MB),
        name="send_blocks",
    )(rows, p_t)


def term_of(pair, doubled):
    applied = jnp.dot(pair[:, :64], doubled, preferred_element_type=F32).astype(BF16)
    term = jnp.dot(pair[:, 64:], applied, preferred_element_type=F32)
    low = lax.broadcasted_iota(jnp.int32, (32, 128), 1) < 64
    return jnp.where(low, term[:32], term[32:])


def near_kernel(me, neighbours, slot, parent, a_ref, r_ref, p_ref, *refs):
    far_pairs_out, sums_out, early_low, early_high, plan_out, pairs, doubled, wide, far_pairs, sums, early = refs[:11]
    plan, near_pairs, near_blocks, near_sums, far_list, written = refs[11:]
    copies = []

    def two(i):
        block = p_ref[rows_at(i, 64), :]
        return jnp.concatenate([block, block], 0)

    transpose_slabs(two, 64, 72, wide)
    doubled[...] = wide[...].reshape(E, 72, 128)[:, :64].astype(BF16)

    @pl.loop(0, 4)
    def _(k):
        transpose_slabs(
            lambda i: jnp.concatenate([a_ref[rows_at(k * 64 + i, 64), :], r_ref[rows_at(i, 64), :]], 0), 64, 72, wide
        )
        pairs[rows_at(k, E)] = wide[...].reshape(E, 72, 128)[:, :64].astype(BF16)

    pairs[4 * E] = jnp.zeros((64, 128), BF16)

    for part, ahead in enumerate(AHEAD):
        first = lax.rem(me[0] + ahead, 4) * SPAN
        start = part * AREA

        def element(i, carry):
            near, far = carry
            e = first + i
            base = lax.rem(parent[0, e], ROWS) * SLOTS
            near_pairs[near] = e
            near_blocks[near] = e
            near_sums[near] = base + slot[0, e]
            near = near + 1
            for k in range(1, 4):
                code = neighbours[k - 1, e]
                block_sum = base + slot[k, e]
                near_pairs[near] = k * E + e
                near_blocks[near] = code
                near_sums[near] = block_sum
                far_list[far] = k * E + e
                plan[far] = code - E
                plan[SUMS + far] = block_sum
                here = (code < E).astype(jnp.int32)
                near = near + here
                far = far + (1 - here)
            return near, far

        near, far = lax.fori_loop(0, SPAN, element, (0, start))
        many = far - start
        plan[COUNTS + part] = many

        def keep(i, carry):
            far_pairs[part, i] = pairs[far_list[start + i]]
            return carry

        lax.fori_loop(0, many, keep, 0)

        def pad_far(i, carry):
            far_pairs[part, i] = jnp.zeros((64, 128), BF16)
            plan[start + i] = 0
            plan[SUMS + start + i] = 0
            return carry

        lax.fori_loop(many, (many + GROUP - 1) // GROUP * GROUP, pad_far, 0)

        def pad_near(i, carry):
            near_pairs[i] = 4 * E
            near_blocks[i] = 0
            near_sums[i] = 0
            return carry

        copies.append(pltpu.make_async_copy(far_pairs.at[part], far_pairs_out.at[part], written.at[part]))
        copies[-1].start()
        groups = (near + GROUP - 1) // GROUP
        lax.fori_loop(near, groups * GROUP, pad_near, 0)
        sums[part] = jnp.zeros((BLOCKS, 32, 128), F32)

        def group(g, carry):
            at = g * GROUP
            found = [term_of(pairs[near_pairs[at + u]], doubled[near_blocks[at + u]]) for u in range(GROUP)]
            for u in range(GROUP):
                sums[part, near_sums[at + u]] += found[u]
            return carry

        lax.fori_loop(0, groups, group, 0)
        if part == 0:
            early[...] = sums[0].astype(BF16)
            for h, out in enumerate((early_low, early_high)):
                copies.append(pltpu.make_async_copy(early.at[pl.ds(h * HALF, HALF)], out, written.at[9 + h]))
                copies[-1].start()
        else:
            copies.append(pltpu.make_async_copy(sums.at[part], sums_out.at[part], written.at[4 + part]))
            copies[-1].start()

    copies.append(pltpu.make_async_copy(plan, plan_out.at[pl.ds(0, PLAN)], written.at[8]))
    copies[-1].start()
    for copy in copies:
        copy.wait()


def near_terms(me, neighbours, slot, parent, a_t, r_t, p_t):
    return pl.pallas_call(
        near_kernel,
        out_shape=[
            jax.ShapeDtypeStruct((4, CAP, 64, 128), BF16),
            jax.ShapeDtypeStruct((4, BLOCKS, 32, 128), F32),
            jax.ShapeDtypeStruct((HALF, 32, 128), BF16),
            jax.ShapeDtypeStruct((HALF, 32, 128), BF16),
        ]
        + [jax.ShapeDtypeStruct((ROOM,), jnp.int32)],
        in_specs=[pl.BlockSpec(memory_space=SM)] * 4 + [pl.BlockSpec(memory_space=VM)] * 3,
        out_specs=[pl.BlockSpec(memory_space=HBM)] * 5,
        scratch_shapes=[
            VM((4 * E + 1, 64, 128), BF16),
            VM((E, 64, 128), BF16),
            VM((E * 72, 128), F32),
            VM((4, CAP, 64, 128), BF16),
            VM((4, BLOCKS, 32, 128), F32),
            VM((BLOCKS, 32, 128), BF16),
            SM((PLAN,), jnp.int32),
            SM((4 * SPAN + GROUP,), jnp.int32),
            SM((4 * SPAN + GROUP,), jnp.int32),
            SM((4 * SPAN + GROUP,), jnp.int32),
            SM((4 * AREA,), jnp.int32),
            pltpu.SemaphoreType.DMA((11,)),
        ],
        compiler_params=pltpu.CompilerParams(vmem_limit_bytes=55 * MB),
        cost_estimate=pl.CostEstimate(flops=700_000_000, bytes_accessed=40_000_000, transcendentals=0),
        name="near_terms",
    )(me, neighbours, slot, parent, a_t, r_t, p_t)


def far_kernel(parts, kinds, plan_in, incoming, *refs):
    pairs_in, near_in, *outs = refs[:-6]
    plan, pairs, near, sums, arrived, plan_arrived = refs[-6:]
    plan_copy = pltpu.make_async_copy(plan_in.at[pl.ds(0, PLAN)], plan, plan_arrived)
    plan_copy.start()
    low = lax.broadcasted_iota(jnp.int32, (32, 128), 1) < 64

    def pairs_copy(n, g):
        some = pl.ds(g * GROUP, GROUP)
        return pltpu.make_async_copy(pairs_in.at[parts[n], some], pairs.at[n, some], arrived.at[n, g])

    def near_copy(n):
        return pltpu.make_async_copy(near_in.at[parts[n]], near.at[n], arrived.at[n, GROUPS])

    def doubled(block):
        x = incoming[block]
        turned = jnp.concatenate([x[:, 64:], x[:, :64]], 1)
        return jnp.concatenate([jnp.where(low, x, turned), jnp.where(low, turned, x)], 0)

    for n in range(len(parts)):
        pairs_copy(n, 0).start()
        if parts[n]:
            near_copy(n).start()
    plan_copy.wait()
    for n, part in enumerate(parts):
        for g in range(1, GROUPS):

            @pl.when(plan[COUNTS + part] > g * GROUP)
            def _(n=n, g=g):
                pairs_copy(n, g).start()


    for n, part in enumerate(parts):
        sums[...] = jnp.zeros_like(sums)
        start = part * AREA
        groups = (plan[COUNTS + part] + GROUP - 1) // GROUP

        def group(g, carry):
            at = g * GROUP
            pairs_copy(n, g).wait()
            found = [term_of(pairs[n, at + u], doubled(plan[start + at + u])) for u in range(GROUP)]
            for u in range(GROUP):
                sums[plan[SUMS + start + at + u]] += found[u]
            return carry

        lax.fori_loop(0, groups, group, 0)

        @pl.when(groups == 0)
        def _(n=n):
            pairs_copy(n, 0).wait()

        if part:
            near_copy(n).wait()
        size = BLOCKS // len(kinds[n])
        for h, kind in enumerate(kinds[n]):
            some = pl.ds(h * size, size)
            total = near[n, some] + sums[some] if part else sums[some]
            outs[2 * n + h][...] = total.astype(kind)


def far_terms(parts, kinds, plan, incoming, pairs, near, name):
    shapes = [(BLOCKS // len(some), kind) for some in kinds for kind in some]
    return pl.pallas_call(
        functools.partial(far_kernel, parts, kinds),
        in_specs=[pl.BlockSpec(memory_space=HBM), pl.BlockSpec(memory_space=VM)]
        + [pl.BlockSpec(memory_space=HBM)] * 2,
        out_specs=[pl.BlockSpec(memory_space=VM)] * len(shapes),
        scratch_shapes=[
            SM((PLAN,), jnp.int32),
            VM((len(parts), CAP, 64, 128), BF16),
            VM((len(parts), BLOCKS, 32, 128), F32),
            VM((BLOCKS, 32, 128), F32),
            pltpu.SemaphoreType.DMA((len(parts), GROUPS + 1)),
            pltpu.SemaphoreType.DMA,
        ],
        out_shape=[jax.ShapeDtypeStruct((size, 32, 128), kind) for size, kind in shapes],
        compiler_params=pltpu.CompilerParams(vmem_limit_bytes=48 * MB),
        cost_estimate=pl.CostEstimate(flops=100_000_000, bytes_accessed=6_000_000, transcendentals=0),
        name=name,
    )(plan, incoming, pairs, near)


def add_kernel(here_a, early_a, passed_a, here_b, early_b, passed_b, *outs):
    sides = (here_a, early_a, passed_a), (here_b, early_b, passed_b)
    for n, (here, early, passed) in enumerate(sides):
        total = (here[...] + early[...].astype(F32) + passed[...].astype(F32)).astype(BF16)
        outs[2 * n][...] = total[:FIRST]
        outs[2 * n + 1][...] = total[FIRST:]


def add_passed(*parts):
    return pl.pallas_call(
        add_kernel,
        out_shape=[jax.ShapeDtypeStruct((size, 32, 128), BF16) for size in (FIRST, HALF - FIRST)] * 2,
        in_specs=[pl.BlockSpec(memory_space=VM)] * 6,
        out_specs=[pl.BlockSpec(memory_space=VM)] * 4,
        compiler_params=pltpu.CompilerParams(vmem_limit_bytes=16 * MB),
        name="add_passed",
    )(*parts)


def finish_kernel(first, size, own, low_a, low_b, high_a, high_b, *refs):
    out_ref, totals, written = refs[-3:]
    copies = []
    step = size // 2
    for h, (one, other) in enumerate(((low_a, low_b), (high_a, high_b))):
        for c in range(2):
            at = first + c * step
            some = pl.ds(h * HALF + at, step)
            mine = pl.ds(h * size + c * step, step)
            total = own[some] + one[pl.ds(at, step)].astype(F32) + other[pl.ds(c * step, step)].astype(F32)
            totals[mine, :32] = total[:, :, :64]
            totals[mine, 32:] = total[:, :, 64:]
            copies.append(pltpu.make_async_copy(totals.at[mine], out_ref.at[some], written.at[2 * h + c]))
            copies[-1].start()
    for copy in copies:
        copy.wait()


def finish(first, size, *parts):
    return pl.pallas_call(
        functools.partial(finish_kernel, first, size),
        out_shape=jax.ShapeDtypeStruct((BLOCKS, 64, 64), F32),
        in_specs=[pl.BlockSpec(memory_space=VM)] * 5 + [pl.BlockSpec(memory_space=HBM)] * (len(parts) - 5),
        out_specs=pl.BlockSpec(memory_space=HBM),
        input_output_aliases={5: 0} if first else {},
        scratch_shapes=[VM((2 * size, 64, 64), F32), pltpu.SemaphoreType.DMA((4,))],
        compiler_params=pltpu.CompilerParams(vmem_limit_bytes=24 * MB),
        name=f"finish_{first}",
    )(*parts)


def on_device(a_blocks, r_blocks, p_blocks, neighbours, send_rows, parent, slot):
    a_t = jnp.transpose(a_blocks, (1, 2, 3, 0)).reshape(4 * 4096, E)
    r_t = jnp.transpose(r_blocks, (1, 2, 0)).reshape(4096, E)
    p_t = jnp.transpose(p_blocks, (1, 2, 0))
    me = lax.axis_index("grp").astype(jnp.int32).reshape(1)
    with jax.named_scope("exchange"):
        outgoing = send_blocks(jnp.transpose(send_rows, (2, 0, 1)), p_t.reshape(2, 32, 64, E))
        incoming = lax.all_to_all(outgoing.reshape(64, 96, 128), "dev", 0, 0, tiled=True).reshape(FAR, 32, 128)
    with jax.named_scope("near"):
        pairs, near, early_low, early_high, plan = near_terms(
            me, neighbours.T, slot.T, parent.reshape(1, E), a_t, r_t, p_t.reshape(4096, E)
        )

    def to_next(x):
        return lax.ppermute(x, "grp", [(i, (i + 1) % 4) for i in range(4)])

    def to_last(x):
        return lax.ppermute(x, "grp", [(i, (i + 3) % 4) for i in range(4)])

    with jax.named_scope("early"):
        early_low, early_high = to_next(early_low), to_last(early_high)
        incoming, early_low, early_high = lax.optimization_barrier((incoming, early_low, early_high))
    with jax.named_scope("far"):
        far_low, far_high = far_terms((0,), ((BF16, BF16),), plan, incoming, pairs, near, "far_two")
        passed_low, passed_high = to_next(far_low), to_last(far_high)
        next_low, next_high, last_low, last_high = far_terms(
            (1, 2), ((F32, BF16), (BF16, F32)), plan, incoming, pairs, near, "far_one"
        )
        from_last_high, from_next_low = to_next(next_high), to_last(last_low)
        low, low_rest, high, high_rest = add_passed(
            next_low, early_low, passed_low, last_high, early_high, passed_high
        )
        from_last_low, from_next_high = to_next(low), to_last(high)
        low_rest, high_rest = to_next(low_rest), to_last(high_rest)
        (own,) = far_terms((3,), ((F32,),), plan, incoming, pairs, near, "far_own")
    with jax.named_scope("finish"):
        coarse = finish(0, FIRST, own, from_next_low, from_last_low, from_last_high, from_next_high)
        coarse = finish(FIRST, HALF - FIRST, own, from_next_low, low_rest, from_last_high, high_rest, coarse)
    return coarse.reshape(ROWS, SLOTS, 64, 64)


def solution(mesh):
    return jax.shard_map(
        on_device,
        mesh=mesh,
        in_specs=(
            P(("grp", "dev"), None, None, None),
            P(("grp", "dev"), None, None),
            P(("grp", "dev"), None, None),
            P(("grp", "dev"), None),
            P(("grp", "dev"), None, None),
            P(("grp", "dev")),
            P(("grp", "dev"), None),
        ),
        out_specs=P(("grp", "dev"), None, None, None),
        check_vma=False,
    )
```

```python
import functools

import jax
import jax.numpy as jnp
from jax import lax
from jax.experimental import pallas as pl
from jax.experimental.pallas import tpu as pltpu
from jax.sharding import PartitionSpec as P

MB = 1 << 20
F32 = jnp.float32
BF16 = jnp.bfloat16
VM = pltpu.VMEM
SM = pltpu.SMEM
HBM = pltpu.HBM

E = 128
SPAN = 32
ROWS = 16
SLOTS = 7
BLOCKS = ROWS * SLOTS
HALF = BLOCKS // 2
FAR = 192
CAP = 3 * SPAN
GROUP = 32
GROUPS = CAP // GROUP
CHUNKS = 4
SURE = 2
FIRST = 40
AREA = CAP + GROUP
SUMS = 4 * AREA
COUNTS = 8 * AREA
PLAN = COUNTS + 1024
NEAR_AREA = 4 * SPAN + GROUP
ROOM = 3 * MB
AHEAD = (2, 1, 3, 0)


def rows_at(index, size):
    return pl.ds(pl.multiple_of(index * size, size), size)


def transpose_slabs(slab_of, steps, stride, wide, first=0):
    @pl.loop(0, steps, unroll=8)
    def _(i):
        wide[pl.ds(first + i, E, stride=stride), :] = slab_of(i).astype(F32).T


def send_kernel(rows, p_ref, out_ref, rows_here, blocks, wide, outgoing, arrived, written):
    rows_copy = pltpu.make_async_copy(rows, rows_here, arrived.at[4])
    rows_copy.start()
    copies = [
        pltpu.make_async_copy(p_ref.at[:, pl.ds(c * 8, 8)], blocks.at[c], arrived.at[c]) for c in range(4)
    ]
    for copy in copies:
        copy.start()
    for c in range(4):
        copies[c].wait()
        transpose_slabs(lambda i: blocks[c, :, i].reshape(128, E), 8, 40, wide, c * 8)
    rows_copy.wait()

    copies = []
    for c in range(CHUNKS):
        size = FAR // CHUNKS

        @pl.loop(0, 64 // CHUNKS, unroll=4)
        def _(n):
            peer = c * (64 // CHUNKS) + n
            for s in range(3):
                row = pl.multiple_of(rows_here[s, 0, peer] * 40, 8)
                outgoing[peer * 3 + s] = wide[pl.ds(row, 32), :].astype(BF16)

        some = pl.ds(c * size, size)
        copies.append(pltpu.make_async_copy(outgoing.at[some], out_ref.at[some], written.at[c]))
        copies[-1].start()
    for copy in copies:
        copy.wait()


def send_blocks(rows, p_t):
    return pl.pallas_call(
        send_kernel,
        out_shape=jax.ShapeDtypeStruct((FAR, 32, 128), BF16),
        in_specs=[pl.BlockSpec(memory_space=HBM)] * 2,
        out_specs=pl.BlockSpec(memory_space=HBM),
        scratch_shapes=[
            SM((3, 1, 64), jnp.int32),
            VM((4, 2, 8, 64, E), BF16),
            VM((E * 40, 128), F32),
            VM((FAR, 32, 128), BF16),
            pltpu.SemaphoreType.DMA((5,)),
            pltpu.SemaphoreType.DMA((CHUNKS,)),
        ],
        compiler_params=pltpu.CompilerParams(vmem_limit_bytes=63 * MB),
        name="send_blocks",
    )(rows, p_t)


def term_of(pair, doubled):
    applied = jnp.dot(pair[:, :64], doubled, preferred_element_type=F32).astype(BF16)
    term = jnp.dot(pair[:, 64:], applied, preferred_element_type=F32)
    low = lax.broadcasted_iota(jnp.int32, (32, 128), 1) < 64
    return jnp.where(low, term[:32], term[32:])


def near_kernel(me, neighbours, slot, parent, a_in, r_in, p_in, *refs):
    far_pairs_out, sums_out, early_low, early_high, plan_out, a_ref, r_ref, p_ref, pairs, doubled = refs[:10]
    wide, far_pairs, sums, early, plan, near_pairs, near_blocks, near_sums, far_list, arrived, written = refs[10:]
    incoming = [pltpu.make_async_copy(p_in, p_ref, arrived.at[5]), pltpu.make_async_copy(r_in, r_ref, arrived.at[4])]
    incoming += [pltpu.make_async_copy(a_in.at[k], a_ref.at[k], arrived.at[k]) for k in range(4)]
    for copy in incoming:
        copy.start()
    copies = []

    near_counts, far_counts = [], []
    for part, ahead in enumerate(AHEAD):
        first = lax.rem(me[0] + ahead, 4) * SPAN

        def element(i, carry):
            near, far = carry
            e = first + i
            base = lax.rem(parent[0, e], ROWS) * SLOTS
            near_pairs[near] = e
            near_blocks[near] = e
            near_sums[near] = base + slot[0, e]
            near = near + 1
            for k in range(1, 4):
                code = neighbours[k - 1, e]
                block_sum = base + slot[k, e]
                near_pairs[near] = k * E + e
                near_blocks[near] = code
                near_sums[near] = block_sum
                far_list[far] = k * E + e
                plan[far] = code - E
                plan[SUMS + far] = block_sum
                here = (code < E).astype(jnp.int32)
                near = near + here
                far = far + (1 - here)
            return near, far

        near, far = lax.fori_loop(0, SPAN, element, (part * NEAR_AREA, part * AREA), unroll=2)
        near_counts.append(near - part * NEAR_AREA)
        far_counts.append(far - part * AREA)
        plan[COUNTS + part] = far_counts[-1]

        def pad_far(i, carry):
            plan[part * AREA + i] = 0
            plan[SUMS + part * AREA + i] = 0
            return carry

        lax.fori_loop(far_counts[-1], (far_counts[-1] + GROUP - 1) // GROUP * GROUP, pad_far, 0)

        def pad_near(i, carry):
            near_pairs[part * NEAR_AREA + i] = 4 * E
            near_blocks[part * NEAR_AREA + i] = 0
            near_sums[part * NEAR_AREA + i] = 0
            return carry

        lax.fori_loop(near_counts[-1], (near_counts[-1] + GROUP - 1) // GROUP * GROUP, pad_near, 0)

    copies.append(pltpu.make_async_copy(plan, plan_out.at[pl.ds(0, PLAN)], written.at[8]))
    copies[-1].start()

    def two(i):
        block = p_ref[rows_at(i, 64), :]
        return jnp.concatenate([block, block], 0)

    incoming[0].wait()
    transpose_slabs(two, 64, 72, wide)
    doubled[...] = wide[...].reshape(E, 72, 128)[:, :64].astype(BF16)
    incoming[1].wait()
    for k in range(4):
        incoming[2 + k].wait()
        transpose_slabs(
            lambda i: jnp.concatenate([a_ref[k, rows_at(i, 64), :], r_ref[rows_at(i, 64), :]], 0), 64, 72, wide
        )
        pairs[rows_at(k, E)] = wide[...].reshape(E, 72, 128)[:, :64].astype(BF16)
    pairs[4 * E] = jnp.zeros((64, 128), BF16)

    for part in range(4):
        start, many = part * AREA, far_counts[part]

        def keep(i, carry):
            far_pairs[part, i] = pairs[far_list[start + i]]
            return carry

        lax.fori_loop(0, many, keep, 0)

        def clear(i, carry):
            far_pairs[part, i] = jnp.zeros((64, 128), BF16)
            return carry

        lax.fori_loop(many, (many + GROUP - 1) // GROUP * GROUP, clear, 0)
        copies.append(pltpu.make_async_copy(far_pairs.at[part], far_pairs_out.at[part], written.at[part]))
        copies[-1].start()
        sums[part] = jnp.zeros((BLOCKS, 32, 128), F32)

        def group(g, carry):
            at = part * NEAR_AREA + g * GROUP
            found = [term_of(pairs[near_pairs[at + u]], doubled[near_blocks[at + u]]) for u in range(GROUP)]
            for u in range(GROUP):
                sums[part, near_sums[at + u]] += found[u]
            return carry

        lax.fori_loop(0, (near_counts[part] + GROUP - 1) // GROUP, group, 0)
        if part == 0:
            early[...] = sums[0].astype(BF16)
            for h, out in enumerate((early_low, early_high)):
                copies.append(pltpu.make_async_copy(early.at[pl.ds(h * HALF, HALF)], out, written.at[9 + h]))
                copies[-1].start()
        else:
            copies.append(pltpu.make_async_copy(sums.at[part], sums_out.at[part], written.at[4 + part]))
            copies[-1].start()

    for copy in copies:
        copy.wait()


def near_terms(me, neighbours, slot, parent, a_t, r_t, p_t):
    return pl.pallas_call(
        near_kernel,
        out_shape=[
            jax.ShapeDtypeStruct((4, CAP, 64, 128), BF16),
            jax.ShapeDtypeStruct((4, BLOCKS, 32, 128), F32),
            jax.ShapeDtypeStruct((HALF, 32, 128), BF16),
            jax.ShapeDtypeStruct((HALF, 32, 128), BF16),
        ]
        + [jax.ShapeDtypeStruct((ROOM,), jnp.int32)],
        in_specs=[pl.BlockSpec(memory_space=SM)] * 4 + [pl.BlockSpec(memory_space=HBM)] * 3,
        out_specs=[pl.BlockSpec(memory_space=HBM)] * 5,
        scratch_shapes=[
            VM((4, 4096, E), BF16),
            VM((4096, E), BF16),
            VM((4096, E), BF16),
            VM((4 * E + 1, 64, 128), BF16),
            VM((E, 64, 128), BF16),
            VM((E * 72, 128), F32),
            VM((4, CAP, 64, 128), BF16),
            VM((4, BLOCKS, 32, 128), F32),
            VM((BLOCKS, 32, 128), BF16),
            SM((PLAN,), jnp.int32),
            SM((4 * NEAR_AREA,), jnp.int32),
            SM((4 * NEAR_AREA,), jnp.int32),
            SM((4 * NEAR_AREA,), jnp.int32),
            SM((4 * AREA,), jnp.int32),
            pltpu.SemaphoreType.DMA((6,)),
            pltpu.SemaphoreType.DMA((11,)),
        ],
        compiler_params=pltpu.CompilerParams(vmem_limit_bytes=55 * MB),
        cost_estimate=pl.CostEstimate(flops=700_000_000, bytes_accessed=40_000_000, transcendentals=0),
        name="near_terms",
    )(me, neighbours, slot, parent, a_t, r_t, p_t)


def far_kernel(parts, kinds, plan_in, incoming, *refs):
    pairs_in, near_in, *outs = refs[:-6]
    plan, pairs, near, sums, arrived, plan_arrived = refs[-6:]
    plan_copy = pltpu.make_async_copy(plan_in.at[pl.ds(0, PLAN)], plan, plan_arrived)
    plan_copy.start()
    low = lax.broadcasted_iota(jnp.int32, (32, 128), 1) < 64

    def pairs_copy(n, g):
        some = pl.ds(g * GROUP, GROUP)
        return pltpu.make_async_copy(pairs_in.at[parts[n], some], pairs.at[n, some], arrived.at[n, g])

    def near_copy(n):
        return pltpu.make_async_copy(near_in.at[parts[n]], near.at[n], arrived.at[n, GROUPS])

    def doubled(block):
        x = incoming[block]
        turned = jnp.concatenate([x[:, 64:], x[:, :64]], 1)
        return jnp.concatenate([jnp.where(low, x, turned), jnp.where(low, turned, x)], 0)

    for n in range(len(parts)):
        for g in range(SURE):
            pairs_copy(n, g).start()
        if parts[n]:
            near_copy(n).start()
    plan_copy.wait()
    for n, part in enumerate(parts):
        for g in range(SURE, GROUPS):

            @pl.when(plan[COUNTS + part] > g * GROUP)
            def _(n=n, g=g):
                pairs_copy(n, g).start()


    for n, part in enumerate(parts):
        sums[...] = jnp.zeros_like(sums)
        start = part * AREA
        groups = (plan[COUNTS + part] + GROUP - 1) // GROUP

        def group(g, carry):
            at = g * GROUP
            pairs_copy(n, g).wait()
            found = [term_of(pairs[n, at + u], doubled(plan[start + at + u])) for u in range(GROUP)]
            for u in range(GROUP):
                sums[plan[SUMS + start + at + u]] += found[u]
            return carry

        lax.fori_loop(0, groups, group, 0)

        for g in range(SURE):

            @pl.when(groups <= g)
            def _(n=n, g=g):
                pairs_copy(n, g).wait()

        if part:
            near_copy(n).wait()
        size = BLOCKS // len(kinds[n])
        for h, kind in enumerate(kinds[n]):
            some = pl.ds(h * size, size)
            total = near[n, some] + sums[some] if part else sums[some]
            outs[2 * n + h][...] = total.astype(kind)


def far_terms(parts, kinds, plan, incoming, pairs, near, name):
    shapes = [(BLOCKS // len(some), kind) for some in kinds for kind in some]
    return pl.pallas_call(
        functools.partial(far_kernel, parts, kinds),
        in_specs=[pl.BlockSpec(memory_space=HBM), pl.BlockSpec(memory_space=VM)]
        + [pl.BlockSpec(memory_space=HBM)] * 2,
        out_specs=[pl.BlockSpec(memory_space=VM)] * len(shapes),
        scratch_shapes=[
            SM((PLAN,), jnp.int32),
            VM((len(parts), CAP, 64, 128), BF16),
            VM((len(parts), BLOCKS, 32, 128), F32),
            VM((BLOCKS, 32, 128), F32),
            pltpu.SemaphoreType.DMA((len(parts), GROUPS + 1)),
            pltpu.SemaphoreType.DMA,
        ],
        out_shape=[jax.ShapeDtypeStruct((size, 32, 128), kind) for size, kind in shapes],
        compiler_params=pltpu.CompilerParams(vmem_limit_bytes=48 * MB),
        cost_estimate=pl.CostEstimate(flops=100_000_000, bytes_accessed=6_000_000, transcendentals=0),
        name=name,
    )(plan, incoming, pairs, near)


def add_kernel(here_a, early_a, passed_a, here_b, early_b, passed_b, *outs):
    sides = (here_a, early_a, passed_a), (here_b, early_b, passed_b)
    for n, (here, early, passed) in enumerate(sides):
        total = (here[...] + early[...].astype(F32) + passed[...].astype(F32)).astype(BF16)
        outs[2 * n][...] = total[:FIRST]
        outs[2 * n + 1][...] = total[FIRST:]


def add_passed(*parts):
    return pl.pallas_call(
        add_kernel,
        out_shape=[jax.ShapeDtypeStruct((size, 32, 128), BF16) for size in (FIRST, HALF - FIRST)] * 2,
        in_specs=[pl.BlockSpec(memory_space=VM)] * 6,
        out_specs=[pl.BlockSpec(memory_space=VM)] * 4,
        compiler_params=pltpu.CompilerParams(vmem_limit_bytes=16 * MB),
        name="add_passed",
    )(*parts)


def finish_kernel(first, size, own, low_a, low_b, high_a, high_b, *refs):
    out_ref, totals, written = refs[-3:]
    copies = []
    step = size // 2
    for h, (one, other) in enumerate(((low_a, low_b), (high_a, high_b))):
        for c in range(2):
            at = first + c * step
            some = pl.ds(h * HALF + at, step)
            mine = pl.ds(h * size + c * step, step)
            total = own[some] + one[pl.ds(at, step)].astype(F32) + other[pl.ds(c * step, step)].astype(F32)
            totals[mine, :32] = total[:, :, :64]
            totals[mine, 32:] = total[:, :, 64:]
            copies.append(pltpu.make_async_copy(totals.at[mine], out_ref.at[some], written.at[2 * h + c]))
            copies[-1].start()
    for copy in copies:
        copy.wait()


def finish(first, size, *parts):
    return pl.pallas_call(
        functools.partial(finish_kernel, first, size),
        out_shape=jax.ShapeDtypeStruct((BLOCKS, 64, 64), F32),
        in_specs=[pl.BlockSpec(memory_space=VM)] * 5 + [pl.BlockSpec(memory_space=HBM)] * (len(parts) - 5),
        out_specs=pl.BlockSpec(memory_space=HBM),
        input_output_aliases={5: 0} if first else {},
        scratch_shapes=[VM((2 * size, 64, 64), F32), pltpu.SemaphoreType.DMA((4,))],
        compiler_params=pltpu.CompilerParams(vmem_limit_bytes=24 * MB),
        name=f"finish_{first}",
    )(*parts)


def on_device(a_blocks, r_blocks, p_blocks, neighbours, send_rows, parent, slot):
    a_t = jnp.transpose(a_blocks, (1, 2, 3, 0)).reshape(4, 4096, E)
    r_t = jnp.transpose(r_blocks, (1, 2, 0)).reshape(4096, E)
    p_t = jnp.transpose(p_blocks, (1, 2, 0))
    me = lax.axis_index("grp").astype(jnp.int32).reshape(1)
    with jax.named_scope("exchange"):
        outgoing = send_blocks(jnp.transpose(send_rows, (2, 0, 1)), p_t.reshape(2, 32, 64, E))
        incoming = lax.all_to_all(outgoing.reshape(64, 96, 128), "dev", 0, 0, tiled=True).reshape(FAR, 32, 128)
    with jax.named_scope("near"):
        pairs, near, early_low, early_high, plan = near_terms(
            me, neighbours.T, slot.T, parent.reshape(1, E), a_t, r_t, p_t.reshape(4096, E)
        )

    def to_next(x):
        return lax.ppermute(x, "grp", [(i, (i + 1) % 4) for i in range(4)])

    def to_last(x):
        return lax.ppermute(x, "grp", [(i, (i + 3) % 4) for i in range(4)])

    with jax.named_scope("early"):
        early_low, early_high = to_next(early_low), to_last(early_high)
    with jax.named_scope("far"):
        far_low, far_high = far_terms((0,), ((BF16, BF16),), plan, incoming, pairs, near, "far_two")
        passed_low, passed_high = to_next(far_low), to_last(far_high)
        next_low, next_high, last_low, last_high = far_terms(
            (1, 2), ((F32, BF16), (BF16, F32)), plan, incoming, pairs, near, "far_one"
        )
        from_last_high, from_next_low = to_next(next_high), to_last(last_low)
        low, low_rest, high, high_rest = add_passed(
            next_low, early_low, passed_low, last_high, early_high, passed_high
        )
        from_last_low, from_next_high = to_next(low), to_last(high)
        low_rest, high_rest = to_next(low_rest), to_last(high_rest)
        (own,) = far_terms((3,), ((F32,),), plan, incoming, pairs, near, "far_own")
    with jax.named_scope("finish"):
        coarse = finish(0, FIRST, own, from_next_low, from_last_low, from_last_high, from_next_high)
        coarse = finish(FIRST, HALF - FIRST, own, from_next_low, low_rest, from_last_high, high_rest, coarse)
    return coarse.reshape(ROWS, SLOTS, 64, 64)


def solution(mesh):
    return jax.shard_map(
        on_device,
        mesh=mesh,
        in_specs=(
            P(("grp", "dev"), None, None, None),
            P(("grp", "dev"), None, None),
            P(("grp", "dev"), None, None),
            P(("grp", "dev"), None),
            P(("grp", "dev"), None, None),
            P(("grp", "dev")),
            P(("grp", "dev"), None),
        ),
        out_specs=P(("grp", "dev"), None, None, None),
        check_vma=False,
    )
```

```python
import functools

import jax
import jax.numpy as jnp
from jax import lax
from jax.experimental import pallas as pl
from jax.experimental.pallas import tpu as pltpu
from jax.sharding import PartitionSpec as P

MB = 1 << 20
F32 = jnp.float32
BF16 = jnp.bfloat16
VM = pltpu.VMEM
SM = pltpu.SMEM
HBM = pltpu.HBM

E = 128
SPAN = 32
ROWS = 16
SLOTS = 7
BLOCKS = ROWS * SLOTS
HALF = BLOCKS // 2
FAR = 192
CAP = 3 * SPAN
GROUP = 32
GROUPS = CAP // GROUP
CHUNKS = 4
SURE = 2
FIRST = 40
AREA = CAP + GROUP
SUMS = 4 * AREA
COUNTS = 8 * AREA
PLAN = COUNTS + 1024
NEAR_AREA = 4 * SPAN + GROUP
ROOM = 3 * MB
AHEAD = (2, 1, 3, 0)


def rows_at(index, size):
    return pl.ds(pl.multiple_of(index * size, size), size)


def transpose_slabs(slab_of, steps, stride, wide, first=0):
    @pl.loop(0, steps, unroll=8)
    def _(i):
        wide[pl.ds(first + i, E, stride=stride), :] = slab_of(i).astype(F32).T


def send_kernel(rows, p_ref, out_ref, rows_here, blocks, wide, outgoing, arrived, written):
    rows_copy = pltpu.make_async_copy(rows, rows_here, arrived.at[4])
    rows_copy.start()
    copies = [
        pltpu.make_async_copy(p_ref.at[:, pl.ds(c * 8, 8)], blocks.at[c], arrived.at[c]) for c in range(4)
    ]
    for copy in copies:
        copy.start()
    for c in range(4):
        copies[c].wait()
        transpose_slabs(lambda i: blocks[c, :, i].reshape(128, E), 8, 40, wide, c * 8)
    rows_copy.wait()

    copies = []
    for c in range(CHUNKS):
        size = FAR // CHUNKS

        @pl.loop(0, 64 // CHUNKS, unroll=4)
        def _(n):
            peer = c * (64 // CHUNKS) + n
            for s in range(3):
                row = pl.multiple_of(rows_here[s, 0, peer] * 40, 8)
                outgoing[peer * 3 + s] = wide[pl.ds(row, 32), :].astype(BF16)

        some = pl.ds(c * size, size)
        copies.append(pltpu.make_async_copy(outgoing.at[some], out_ref.at[some], written.at[c]))
        copies[-1].start()
    for copy in copies:
        copy.wait()


def send_blocks(rows, p_t):
    return pl.pallas_call(
        send_kernel,
        out_shape=jax.ShapeDtypeStruct((FAR, 32, 128), BF16),
        in_specs=[pl.BlockSpec(memory_space=HBM)] * 2,
        out_specs=pl.BlockSpec(memory_space=HBM),
        scratch_shapes=[
            SM((3, 1, 64), jnp.int32),
            VM((4, 2, 8, 64, E), BF16),
            VM((E * 40 + 40, 128), F32),
            VM((FAR, 32, 128), BF16),
            pltpu.SemaphoreType.DMA((5,)),
            pltpu.SemaphoreType.DMA((CHUNKS,)),
        ],
        compiler_params=pltpu.CompilerParams(vmem_limit_bytes=63 * MB),
        name="send_blocks",
    )(rows, p_t)


def term_of(pair, doubled):
    applied = jnp.dot(pair[:, :64], doubled, preferred_element_type=F32).astype(BF16)
    term = jnp.dot(pair[:, 64:], applied, preferred_element_type=F32)
    low = lax.broadcasted_iota(jnp.int32, (32, 128), 1) < 64
    return jnp.where(low, term[:32], term[32:])


def near_kernel(me, neighbours, slot, parent, a_in, r_in, p_in, *refs):
    far_pairs_out, sums_out, early_low, early_high, plan_out, a_ref, r_ref, p_ref, pairs, doubled = refs[:10]
    wide, far_pairs, sums, early, plan, near_pairs, near_blocks, near_sums, far_list, arrived, written = refs[10:]
    incoming = [pltpu.make_async_copy(p_in, p_ref, arrived.at[5]), pltpu.make_async_copy(r_in, r_ref, arrived.at[4])]
    incoming += [pltpu.make_async_copy(a_in.at[k], a_ref.at[k], arrived.at[k]) for k in range(4)]
    for copy in incoming:
        copy.start()
    copies = []

    near_counts, far_counts = [], []
    for part, ahead in enumerate(AHEAD):
        first = lax.rem(me[0] + ahead, 4) * SPAN

        def element(i, carry):
            near, far = carry
            e = first + i
            base = lax.rem(parent[0, e], ROWS) * SLOTS
            near_pairs[near] = e
            near_blocks[near] = e
            near_sums[near] = base + slot[0, e]
            near = near + 1
            for k in range(1, 4):
                code = neighbours[k - 1, e]
                block_sum = base + slot[k, e]
                near_pairs[near] = k * E + e
                near_blocks[near] = code
                near_sums[near] = block_sum
                far_list[far] = k * E + e
                plan[far] = code - E
                plan[SUMS + far] = block_sum
                here = (code < E).astype(jnp.int32)
                near = near + here
                far = far + (1 - here)
            return near, far

        near, far = lax.fori_loop(0, SPAN, element, (part * NEAR_AREA, part * AREA), unroll=2)
        near_counts.append(near - part * NEAR_AREA)
        far_counts.append(far - part * AREA)
        plan[COUNTS + part] = far_counts[-1]

        def pad_far(i, carry):
            plan[part * AREA + i] = 0
            plan[SUMS + part * AREA + i] = 0
            return carry

        lax.fori_loop(far_counts[-1], (far_counts[-1] + GROUP - 1) // GROUP * GROUP, pad_far, 0)

        def pad_near(i, carry):
            near_pairs[part * NEAR_AREA + i] = 4 * E
            near_blocks[part * NEAR_AREA + i] = 0
            near_sums[part * NEAR_AREA + i] = 0
            return carry

        lax.fori_loop(near_counts[-1], (near_counts[-1] + GROUP - 1) // GROUP * GROUP, pad_near, 0)

    copies.append(pltpu.make_async_copy(plan, plan_out.at[pl.ds(0, PLAN)], written.at[8]))
    copies[-1].start()

    def two(i):
        block = p_ref[rows_at(i, 64), :]
        return jnp.concatenate([block, block], 0)

    incoming[0].wait()
    transpose_slabs(two, 64, 72, wide)
    doubled[...] = wide[: E * 72].reshape(E, 72, 128)[:, :64].astype(BF16)
    incoming[1].wait()
    for k in range(4):
        incoming[2 + k].wait()
        transpose_slabs(
            lambda i: jnp.concatenate([a_ref[k, rows_at(i, 64), :], r_ref[rows_at(i, 64), :]], 0), 64, 72, wide
        )
        pairs[rows_at(k, E)] = wide[: E * 72].reshape(E, 72, 128)[:, :64].astype(BF16)
    pairs[4 * E] = jnp.zeros((64, 128), BF16)

    for part in range(4):
        start, many = part * AREA, far_counts[part]

        def keep(i, carry):
            far_pairs[part, i] = pairs[far_list[start + i]]
            return carry

        lax.fori_loop(0, many, keep, 0)

        def clear(i, carry):
            far_pairs[part, i] = jnp.zeros((64, 128), BF16)
            return carry

        lax.fori_loop(many, (many + GROUP - 1) // GROUP * GROUP, clear, 0)
        copies.append(pltpu.make_async_copy(far_pairs.at[part], far_pairs_out.at[part], written.at[part]))
        copies[-1].start()
        sums[part] = jnp.zeros((BLOCKS, 32, 128), F32)

        def group(g, carry):
            at = part * NEAR_AREA + g * GROUP
            found = [term_of(pairs[near_pairs[at + u]], doubled[near_blocks[at + u]]) for u in range(GROUP)]
            for u in range(GROUP):
                sums[part, near_sums[at + u]] += found[u]
            return carry

        lax.fori_loop(0, (near_counts[part] + GROUP - 1) // GROUP, group, 0)
        if part == 0:
            early[...] = sums[0].astype(BF16)
            for h, out in enumerate((early_low, early_high)):
                copies.append(pltpu.make_async_copy(early.at[pl.ds(h * HALF, HALF)], out, written.at[9 + h]))
                copies[-1].start()
        else:
            copies.append(pltpu.make_async_copy(sums.at[part], sums_out.at[part], written.at[4 + part]))
            copies[-1].start()

    for copy in copies:
        copy.wait()


def near_terms(me, neighbours, slot, parent, a_t, r_t, p_t):
    return pl.pallas_call(
        near_kernel,
        out_shape=[
            jax.ShapeDtypeStruct((4, CAP, 64, 128), BF16),
            jax.ShapeDtypeStruct((4, BLOCKS, 32, 128), F32),
            jax.ShapeDtypeStruct((HALF, 32, 128), BF16),
            jax.ShapeDtypeStruct((HALF, 32, 128), BF16),
        ]
        + [jax.ShapeDtypeStruct((ROOM,), jnp.int32)],
        in_specs=[pl.BlockSpec(memory_space=SM)] * 4 + [pl.BlockSpec(memory_space=HBM)] * 3,
        out_specs=[pl.BlockSpec(memory_space=HBM)] * 5,
        scratch_shapes=[
            VM((4, 4096, E), BF16),
            VM((4096, E), BF16),
            VM((4096, E), BF16),
            VM((4 * E + 1, 64, 128), BF16),
            VM((E, 64, 128), BF16),
            VM((E * 72 + 72, 128), F32),
            VM((4, CAP, 64, 128), BF16),
            VM((4, BLOCKS, 32, 128), F32),
            VM((BLOCKS, 32, 128), BF16),
            SM((PLAN,), jnp.int32),
            SM((4 * NEAR_AREA,), jnp.int32),
            SM((4 * NEAR_AREA,), jnp.int32),
            SM((4 * NEAR_AREA,), jnp.int32),
            SM((4 * AREA,), jnp.int32),
            pltpu.SemaphoreType.DMA((6,)),
            pltpu.SemaphoreType.DMA((11,)),
        ],
        compiler_params=pltpu.CompilerParams(vmem_limit_bytes=55 * MB),
        cost_estimate=pl.CostEstimate(flops=700_000_000, bytes_accessed=40_000_000, transcendentals=0),
        name="near_terms",
    )(me, neighbours, slot, parent, a_t, r_t, p_t)


def far_kernel(parts, kinds, plan_in, incoming, *refs):
    pairs_in, near_in, *outs = refs[:-6]
    plan, pairs, near, sums, arrived, plan_arrived = refs[-6:]
    plan_copy = pltpu.make_async_copy(plan_in.at[pl.ds(0, PLAN)], plan, plan_arrived)
    plan_copy.start()
    low = lax.broadcasted_iota(jnp.int32, (32, 128), 1) < 64

    def pairs_copy(n, g):
        some = pl.ds(g * GROUP, GROUP)
        return pltpu.make_async_copy(pairs_in.at[parts[n], some], pairs.at[n, some], arrived.at[n, g])

    def near_copy(n):
        return pltpu.make_async_copy(near_in.at[parts[n]], near.at[n], arrived.at[n, GROUPS])

    def doubled(block):
        x = incoming[block]
        turned = jnp.concatenate([x[:, 64:], x[:, :64]], 1)
        return jnp.concatenate([jnp.where(low, x, turned), jnp.where(low, turned, x)], 0)

    for n in range(len(parts)):
        for g in range(SURE):
            pairs_copy(n, g).start()
        if parts[n]:
            near_copy(n).start()
    plan_copy.wait()
    for n, part in enumerate(parts):
        for g in range(SURE, GROUPS):

            @pl.when(plan[COUNTS + part] > g * GROUP)
            def _(n=n, g=g):
                pairs_copy(n, g).start()


    for n, part in enumerate(parts):
        sums[...] = jnp.zeros_like(sums)
        start = part * AREA
        groups = (plan[COUNTS + part] + GROUP - 1) // GROUP

        def group(g, carry):
            at = g * GROUP
            pairs_copy(n, g).wait()
            found = [term_of(pairs[n, at + u], doubled(plan[start + at + u])) for u in range(GROUP)]
            for u in range(GROUP):
                sums[plan[SUMS + start + at + u]] += found[u]
            return carry

        lax.fori_loop(0, groups, group, 0)

        for g in range(SURE):

            @pl.when(groups <= g)
            def _(n=n, g=g):
                pairs_copy(n, g).wait()

        if part:
            near_copy(n).wait()
        size = BLOCKS // len(kinds[n])
        for h, kind in enumerate(kinds[n]):
            some = pl.ds(h * size, size)
            total = near[n, some] + sums[some] if part else sums[some]
            outs[2 * n + h][...] = total.astype(kind)


def far_terms(parts, kinds, plan, incoming, pairs, near, name):
    shapes = [(BLOCKS // len(some), kind) for some in kinds for kind in some]
    return pl.pallas_call(
        functools.partial(far_kernel, parts, kinds),
        in_specs=[pl.BlockSpec(memory_space=HBM), pl.BlockSpec(memory_space=VM)]
        + [pl.BlockSpec(memory_space=HBM)] * 2,
        out_specs=[pl.BlockSpec(memory_space=VM)] * len(shapes),
        scratch_shapes=[
            SM((PLAN,), jnp.int32),
            VM((len(parts), CAP, 64, 128), BF16),
            VM((len(parts), BLOCKS, 32, 128), F32),
            VM((BLOCKS, 32, 128), F32),
            pltpu.SemaphoreType.DMA((len(parts), GROUPS + 1)),
            pltpu.SemaphoreType.DMA,
        ],
        out_shape=[jax.ShapeDtypeStruct((size, 32, 128), kind) for size, kind in shapes],
        compiler_params=pltpu.CompilerParams(vmem_limit_bytes=48 * MB),
        cost_estimate=pl.CostEstimate(flops=100_000_000, bytes_accessed=6_000_000, transcendentals=0),
        name=name,
    )(plan, incoming, pairs, near)


def add_kernel(here_a, early_a, passed_a, here_b, early_b, passed_b, *outs):
    sides = (here_a, early_a, passed_a), (here_b, early_b, passed_b)
    for n, (here, early, passed) in enumerate(sides):
        total = (here[...] + early[...].astype(F32) + passed[...].astype(F32)).astype(BF16)
        outs[2 * n][...] = total[:FIRST]
        outs[2 * n + 1][...] = total[FIRST:]


def add_passed(*parts):
    return pl.pallas_call(
        add_kernel,
        out_shape=[jax.ShapeDtypeStruct((size, 32, 128), BF16) for size in (FIRST, HALF - FIRST)] * 2,
        in_specs=[pl.BlockSpec(memory_space=VM)] * 6,
        out_specs=[pl.BlockSpec(memory_space=VM)] * 4,
        compiler_params=pltpu.CompilerParams(vmem_limit_bytes=16 * MB),
        name="add_passed",
    )(*parts)


def finish_kernel(first, size, own, low_a, low_b, high_a, high_b, *refs):
    out_ref, totals, written = refs[-3:]
    copies = []
    step = size // 2
    for h, (one, other) in enumerate(((low_a, low_b), (high_a, high_b))):
        for c in range(2):
            at = first + c * step
            some = pl.ds(h * HALF + at, step)
            mine = pl.ds(h * size + c * step, step)
            total = own[some] + one[pl.ds(at, step)].astype(F32) + other[pl.ds(c * step, step)].astype(F32)
            totals[mine, :32] = total[:, :, :64]
            totals[mine, 32:] = total[:, :, 64:]
            copies.append(pltpu.make_async_copy(totals.at[mine], out_ref.at[some], written.at[2 * h + c]))
            copies[-1].start()
    for copy in copies:
        copy.wait()


def finish(first, size, *parts):
    return pl.pallas_call(
        functools.partial(finish_kernel, first, size),
        out_shape=jax.ShapeDtypeStruct((BLOCKS, 64, 64), F32),
        in_specs=[pl.BlockSpec(memory_space=VM)] * 5 + [pl.BlockSpec(memory_space=HBM)] * (len(parts) - 5),
        out_specs=pl.BlockSpec(memory_space=HBM),
        input_output_aliases={5: 0} if first else {},
        scratch_shapes=[VM((2 * size, 64, 64), F32), pltpu.SemaphoreType.DMA((4,))],
        compiler_params=pltpu.CompilerParams(vmem_limit_bytes=24 * MB),
        name=f"finish_{first}",
    )(*parts)


def on_device(a_blocks, r_blocks, p_blocks, neighbours, send_rows, parent, slot):
    a_t = jnp.transpose(a_blocks, (1, 2, 3, 0)).reshape(4, 4096, E)
    r_t = jnp.transpose(r_blocks, (1, 2, 0)).reshape(4096, E)
    p_t = jnp.transpose(p_blocks, (1, 2, 0))
    me = lax.axis_index("grp").astype(jnp.int32).reshape(1)
    with jax.named_scope("exchange"):
        outgoing = send_blocks(jnp.transpose(send_rows, (2, 0, 1)), p_t.reshape(2, 32, 64, E))
        incoming = lax.all_to_all(outgoing.reshape(64, 96, 128), "dev", 0, 0, tiled=True).reshape(FAR, 32, 128)
    with jax.named_scope("near"):
        pairs, near, early_low, early_high, plan = near_terms(
            me, neighbours.T, slot.T, parent.reshape(1, E), a_t, r_t, p_t.reshape(4096, E)
        )

    def to_next(x):
        return lax.ppermute(x, "grp", [(i, (i + 1) % 4) for i in range(4)])

    def to_last(x):
        return lax.ppermute(x, "grp", [(i, (i + 3) % 4) for i in range(4)])

    with jax.named_scope("early"):
        early_low, early_high = to_next(early_low), to_last(early_high)
    with jax.named_scope("far"):
        far_low, far_high = far_terms((0,), ((BF16, BF16),), plan, incoming, pairs, near, "far_two")
        passed_low, passed_high = to_next(far_low), to_last(far_high)
        next_low, next_high, last_low, last_high = far_terms(
            (1, 2), ((F32, BF16), (BF16, F32)), plan, incoming, pairs, near, "far_one"
        )
        from_last_high, from_next_low = to_next(next_high), to_last(last_low)
        low, low_rest, high, high_rest = add_passed(
            next_low, early_low, passed_low, last_high, early_high, passed_high
        )
        from_last_low, from_next_high = to_next(low), to_last(high)
        low_rest, high_rest = to_next(low_rest), to_last(high_rest)
        (own,) = far_terms((3,), ((F32,),), plan, incoming, pairs, near, "far_own")
    with jax.named_scope("finish"):
        coarse = finish(0, FIRST, own, from_next_low, from_last_low, from_last_high, from_next_high)
        coarse = finish(FIRST, HALF - FIRST, own, from_next_low, low_rest, from_last_high, high_rest, coarse)
    return coarse.reshape(ROWS, SLOTS, 64, 64)


def solution(mesh):
    return jax.shard_map(
        on_device,
        mesh=mesh,
        in_specs=(
            P(("grp", "dev"), None, None, None),
            P(("grp", "dev"), None, None),
            P(("grp", "dev"), None, None),
            P(("grp", "dev"), None),
            P(("grp", "dev"), None, None),
            P(("grp", "dev")),
            P(("grp", "dev"), None),
        ),
        out_specs=P(("grp", "dev"), None, None, None),
        check_vma=False,
    )
```

```python
import functools

import jax
import jax.numpy as jnp
from jax import lax
from jax.experimental import pallas as pl
from jax.experimental.pallas import tpu as pltpu
from jax.sharding import PartitionSpec as P

MB = 1 << 20
F32 = jnp.float32
BF16 = jnp.bfloat16
VM = pltpu.VMEM
SM = pltpu.SMEM
HBM = pltpu.HBM

E = 128
SPAN = 32
ROWS = 16
SLOTS = 7
BLOCKS = ROWS * SLOTS
HALF = BLOCKS // 2
FAR = 192
CAP = 128
GROUP = 32
FAR_GROUP = 64
GROUPS = CAP // FAR_GROUP
CHUNKS = 4
SURE = 1
FIRST = 40
AREA = CAP
SUMS = 4 * AREA
COUNTS = 8 * AREA
PLAN = COUNTS + 1024
NEAR_AREA = 4 * SPAN + GROUP
ROOM = 3 * MB
AHEAD = (2, 1, 3, 0)


def rows_at(index, size):
    return pl.ds(pl.multiple_of(index * size, size), size)


def transpose_slabs(slab_of, steps, stride, wide, first=0):
    @pl.loop(0, steps, unroll=8)
    def _(i):
        wide[pl.ds(first + i, E, stride=stride), :] = slab_of(i).astype(F32).T


def send_kernel(rows, p_ref, out_ref, rows_here, blocks, wide, outgoing, arrived, written):
    rows_copy = pltpu.make_async_copy(rows, rows_here, arrived.at[4])
    rows_copy.start()
    copies = [
        pltpu.make_async_copy(p_ref.at[:, pl.ds(c * 8, 8)], blocks.at[c], arrived.at[c]) for c in range(4)
    ]
    for copy in copies:
        copy.start()
    for c in range(4):
        copies[c].wait()
        transpose_slabs(lambda i: blocks[c, :, i].reshape(128, E), 8, 40, wide, c * 8)
    rows_copy.wait()

    copies = []
    for c in range(CHUNKS):
        size = FAR // CHUNKS

        @pl.loop(0, 64 // CHUNKS, unroll=4)
        def _(n):
            peer = c * (64 // CHUNKS) + n
            for s in range(3):
                row = pl.multiple_of(rows_here[s, 0, peer] * 40, 8)
                outgoing[peer * 3 + s] = wide[pl.ds(row, 32), :].astype(BF16)

        some = pl.ds(c * size, size)
        copies.append(pltpu.make_async_copy(outgoing.at[some], out_ref.at[some], written.at[c]))
        copies[-1].start()
    for copy in copies:
        copy.wait()


def send_blocks(rows, p_t):
    return pl.pallas_call(
        send_kernel,
        out_shape=jax.ShapeDtypeStruct((FAR, 32, 128), BF16),
        in_specs=[pl.BlockSpec(memory_space=HBM)] * 2,
        out_specs=pl.BlockSpec(memory_space=HBM),
        scratch_shapes=[
            SM((3, 1, 64), jnp.int32),
            VM((4, 2, 8, 64, E), BF16),
            VM((E * 40 + 40, 128), F32),
            VM((FAR, 32, 128), BF16),
            pltpu.SemaphoreType.DMA((5,)),
            pltpu.SemaphoreType.DMA((CHUNKS,)),
        ],
        compiler_params=pltpu.CompilerParams(vmem_limit_bytes=63 * MB),
        name="send_blocks",
    )(rows, p_t)


def term_of(pair, doubled):
    applied = jnp.dot(pair[:, :64], doubled, preferred_element_type=F32).astype(BF16)
    term = jnp.dot(pair[:, 64:], applied, preferred_element_type=F32)
    low = lax.broadcasted_iota(jnp.int32, (32, 128), 1) < 64
    return jnp.where(low, term[:32], term[32:])


def near_kernel(me, neighbours, slot, parent, a_in, r_in, p_in, *refs):
    far_pairs_out, sums_out, early_low, early_high, plan_out, a_ref, r_ref, p_ref, pairs, doubled = refs[:10]
    wide, far_pairs, sums, early, plan, near_pairs, near_blocks, near_sums, far_list, arrived, written = refs[10:]
    incoming = [pltpu.make_async_copy(p_in, p_ref, arrived.at[5]), pltpu.make_async_copy(r_in, r_ref, arrived.at[4])]
    incoming += [pltpu.make_async_copy(a_in.at[k], a_ref.at[k], arrived.at[k]) for k in range(4)]
    for copy in incoming:
        copy.start()
    copies = []

    near_counts, far_counts = [], []
    for part, ahead in enumerate(AHEAD):
        first = lax.rem(me[0] + ahead, 4) * SPAN

        def element(i, carry):
            near, far = carry
            e = first + i
            base = lax.rem(parent[0, e], ROWS) * SLOTS
            near_pairs[near] = e
            near_blocks[near] = e
            near_sums[near] = base + slot[0, e]
            near = near + 1
            for k in range(1, 4):
                code = neighbours[k - 1, e]
                block_sum = base + slot[k, e]
                near_pairs[near] = k * E + e
                near_blocks[near] = code
                near_sums[near] = block_sum
                far_list[far] = k * E + e
                plan[far] = code - E
                plan[SUMS + far] = block_sum
                here = (code < E).astype(jnp.int32)
                near = near + here
                far = far + (1 - here)
            return near, far

        near, far = lax.fori_loop(0, SPAN, element, (part * NEAR_AREA, part * AREA), unroll=2)
        near_counts.append(near - part * NEAR_AREA)
        far_counts.append(far - part * AREA)
        plan[COUNTS + part] = far_counts[-1]

        def pad_far(i, carry):
            plan[part * AREA + i] = 0
            plan[SUMS + part * AREA + i] = 0
            return carry

        lax.fori_loop(far_counts[-1], (far_counts[-1] + FAR_GROUP - 1) // FAR_GROUP * FAR_GROUP, pad_far, 0)

        def pad_near(i, carry):
            near_pairs[part * NEAR_AREA + i] = 4 * E
            near_blocks[part * NEAR_AREA + i] = 0
            near_sums[part * NEAR_AREA + i] = 0
            return carry

        lax.fori_loop(near_counts[-1], (near_counts[-1] + GROUP - 1) // GROUP * GROUP, pad_near, 0)

    copies.append(pltpu.make_async_copy(plan, plan_out.at[pl.ds(0, PLAN)], written.at[8]))
    copies[-1].start()

    def two(i):
        block = p_ref[rows_at(i, 64), :]
        return jnp.concatenate([block, block], 0)

    incoming[0].wait()
    transpose_slabs(two, 64, 72, wide)
    doubled[...] = wide[: E * 72].reshape(E, 72, 128)[:, :64].astype(BF16)
    incoming[1].wait()
    for k in range(4):
        incoming[2 + k].wait()
        transpose_slabs(
            lambda i: jnp.concatenate([a_ref[k, rows_at(i, 64), :], r_ref[rows_at(i, 64), :]], 0), 64, 72, wide
        )
        pairs[rows_at(k, E)] = wide[: E * 72].reshape(E, 72, 128)[:, :64].astype(BF16)
    pairs[4 * E] = jnp.zeros((64, 128), BF16)

    for part in range(4):
        start, many = part * AREA, far_counts[part]

        def keep(i, carry):
            far_pairs[part, i] = pairs[far_list[start + i]]
            return carry

        lax.fori_loop(0, many, keep, 0)

        def clear(i, carry):
            far_pairs[part, i] = jnp.zeros((64, 128), BF16)
            return carry

        lax.fori_loop(many, (many + FAR_GROUP - 1) // FAR_GROUP * FAR_GROUP, clear, 0)
        copies.append(pltpu.make_async_copy(far_pairs.at[part], far_pairs_out.at[part], written.at[part]))
        copies[-1].start()
        sums[part] = jnp.zeros((BLOCKS, 32, 128), F32)

        def group(g, carry):
            at = part * NEAR_AREA + g * GROUP
            found = [term_of(pairs[near_pairs[at + u]], doubled[near_blocks[at + u]]) for u in range(GROUP)]
            for u in range(GROUP):
                sums[part, near_sums[at + u]] += found[u]
            return carry

        lax.fori_loop(0, (near_counts[part] + GROUP - 1) // GROUP, group, 0)
        if part == 0:
            early[...] = sums[0].astype(BF16)
            for h, out in enumerate((early_low, early_high)):
                copies.append(pltpu.make_async_copy(early.at[pl.ds(h * HALF, HALF)], out, written.at[9 + h]))
                copies[-1].start()
        else:
            copies.append(pltpu.make_async_copy(sums.at[part], sums_out.at[part], written.at[4 + part]))
            copies[-1].start()

    for copy in copies:
        copy.wait()


def near_terms(me, neighbours, slot, parent, a_t, r_t, p_t):
    return pl.pallas_call(
        near_kernel,
        out_shape=[
            jax.ShapeDtypeStruct((4, CAP, 64, 128), BF16),
            jax.ShapeDtypeStruct((4, BLOCKS, 32, 128), F32),
            jax.ShapeDtypeStruct((HALF, 32, 128), BF16),
            jax.ShapeDtypeStruct((HALF, 32, 128), BF16),
        ]
        + [jax.ShapeDtypeStruct((ROOM,), jnp.int32)],
        in_specs=[pl.BlockSpec(memory_space=SM)] * 4 + [pl.BlockSpec(memory_space=HBM)] * 3,
        out_specs=[pl.BlockSpec(memory_space=HBM)] * 5,
        scratch_shapes=[
            VM((4, 4096, E), BF16),
            VM((4096, E), BF16),
            VM((4096, E), BF16),
            VM((4 * E + 1, 64, 128), BF16),
            VM((E, 64, 128), BF16),
            VM((E * 72 + 72, 128), F32),
            VM((4, CAP, 64, 128), BF16),
            VM((4, BLOCKS, 32, 128), F32),
            VM((BLOCKS, 32, 128), BF16),
            SM((PLAN,), jnp.int32),
            SM((4 * NEAR_AREA,), jnp.int32),
            SM((4 * NEAR_AREA,), jnp.int32),
            SM((4 * NEAR_AREA,), jnp.int32),
            SM((4 * AREA,), jnp.int32),
            pltpu.SemaphoreType.DMA((6,)),
            pltpu.SemaphoreType.DMA((11,)),
        ],
        compiler_params=pltpu.CompilerParams(vmem_limit_bytes=55 * MB),
        cost_estimate=pl.CostEstimate(flops=700_000_000, bytes_accessed=40_000_000, transcendentals=0),
        name="near_terms",
    )(me, neighbours, slot, parent, a_t, r_t, p_t)


def far_kernel(parts, kinds, plan_in, incoming, *refs):
    pairs_in, near_in, *outs = refs[:-6]
    plan, pairs, near, sums, arrived, plan_arrived = refs[-6:]
    plan_copy = pltpu.make_async_copy(plan_in.at[pl.ds(0, PLAN)], plan, plan_arrived)
    plan_copy.start()
    low = lax.broadcasted_iota(jnp.int32, (32, 128), 1) < 64

    def pairs_copy(n, g):
        some = pl.ds(g * FAR_GROUP, FAR_GROUP)
        return pltpu.make_async_copy(pairs_in.at[parts[n], some], pairs.at[n, some], arrived.at[n, g])

    def near_copy(n):
        return pltpu.make_async_copy(near_in.at[parts[n]], near.at[n], arrived.at[n, GROUPS])

    def doubled(block):
        x = incoming[block]
        turned = jnp.concatenate([x[:, 64:], x[:, :64]], 1)
        return jnp.concatenate([jnp.where(low, x, turned), jnp.where(low, turned, x)], 0)

    for n in range(len(parts)):
        for g in range(SURE):
            pairs_copy(n, g).start()
        if parts[n]:
            near_copy(n).start()
    plan_copy.wait()
    for n, part in enumerate(parts):
        for g in range(SURE, GROUPS):

            @pl.when(plan[COUNTS + part] > g * FAR_GROUP)
            def _(n=n, g=g):
                pairs_copy(n, g).start()


    for n, part in enumerate(parts):
        sums[...] = jnp.zeros_like(sums)
        start = part * AREA
        groups = (plan[COUNTS + part] + FAR_GROUP - 1) // FAR_GROUP

        def group(g, carry):
            at = g * FAR_GROUP
            pairs_copy(n, g).wait()
            found = [term_of(pairs[n, at + u], doubled(plan[start + at + u])) for u in range(FAR_GROUP)]
            for u in range(FAR_GROUP):
                sums[plan[SUMS + start + at + u]] += found[u]
            return carry

        lax.fori_loop(0, groups, group, 0)

        for g in range(SURE):

            @pl.when(groups <= g)
            def _(n=n, g=g):
                pairs_copy(n, g).wait()

        if part:
            near_copy(n).wait()
        size = BLOCKS // len(kinds[n])
        for h, kind in enumerate(kinds[n]):
            some = pl.ds(h * size, size)
            total = near[n, some] + sums[some] if part else sums[some]
            outs[2 * n + h][...] = total.astype(kind)


def far_terms(parts, kinds, plan, incoming, pairs, near, name):
    shapes = [(BLOCKS // len(some), kind) for some in kinds for kind in some]
    return pl.pallas_call(
        functools.partial(far_kernel, parts, kinds),
        in_specs=[pl.BlockSpec(memory_space=HBM), pl.BlockSpec(memory_space=VM)]
        + [pl.BlockSpec(memory_space=HBM)] * 2,
        out_specs=[pl.BlockSpec(memory_space=VM)] * len(shapes),
        scratch_shapes=[
            SM((PLAN,), jnp.int32),
            VM((len(parts), CAP, 64, 128), BF16),
            VM((len(parts), BLOCKS, 32, 128), F32),
            VM((BLOCKS, 32, 128), F32),
            pltpu.SemaphoreType.DMA((len(parts), GROUPS + 1)),
            pltpu.SemaphoreType.DMA,
        ],
        out_shape=[jax.ShapeDtypeStruct((size, 32, 128), kind) for size, kind in shapes],
        compiler_params=pltpu.CompilerParams(vmem_limit_bytes=48 * MB),
        cost_estimate=pl.CostEstimate(flops=100_000_000, bytes_accessed=6_000_000, transcendentals=0),
        name=name,
    )(plan, incoming, pairs, near)


def add_kernel(here_a, early_a, passed_a, here_b, early_b, passed_b, *outs):
    sides = (here_a, early_a, passed_a), (here_b, early_b, passed_b)
    for n, (here, early, passed) in enumerate(sides):
        total = (here[...] + early[...].astype(F32) + passed[...].astype(F32)).astype(BF16)
        outs[2 * n][...] = total[:FIRST]
        outs[2 * n + 1][...] = total[FIRST:]


def add_passed(*parts):
    return pl.pallas_call(
        add_kernel,
        out_shape=[jax.ShapeDtypeStruct((size, 32, 128), BF16) for size in (FIRST, HALF - FIRST)] * 2,
        in_specs=[pl.BlockSpec(memory_space=VM)] * 6,
        out_specs=[pl.BlockSpec(memory_space=VM)] * 4,
        compiler_params=pltpu.CompilerParams(vmem_limit_bytes=16 * MB),
        name="add_passed",
    )(*parts)


def finish_kernel(first, size, own, low_a, low_b, high_a, high_b, *refs):
    out_ref, totals, written = refs[-3:]
    copies = []
    step = size // 2
    for h, (one, other) in enumerate(((low_a, low_b), (high_a, high_b))):
        for c in range(2):
            at = first + c * step
            some = pl.ds(h * HALF + at, step)
            mine = pl.ds(h * size + c * step, step)
            total = own[some] + one[pl.ds(at, step)].astype(F32) + other[pl.ds(c * step, step)].astype(F32)
            totals[mine, :32] = total[:, :, :64]
            totals[mine, 32:] = total[:, :, 64:]
            copies.append(pltpu.make_async_copy(totals.at[mine], out_ref.at[some], written.at[2 * h + c]))
            copies[-1].start()
    for copy in copies:
        copy.wait()


def finish(first, size, *parts):
    return pl.pallas_call(
        functools.partial(finish_kernel, first, size),
        out_shape=jax.ShapeDtypeStruct((BLOCKS, 64, 64), F32),
        in_specs=[pl.BlockSpec(memory_space=VM)] * 5 + [pl.BlockSpec(memory_space=HBM)] * (len(parts) - 5),
        out_specs=pl.BlockSpec(memory_space=HBM),
        input_output_aliases={5: 0} if first else {},
        scratch_shapes=[VM((2 * size, 64, 64), F32), pltpu.SemaphoreType.DMA((4,))],
        compiler_params=pltpu.CompilerParams(vmem_limit_bytes=24 * MB),
        name=f"finish_{first}",
    )(*parts)


def on_device(a_blocks, r_blocks, p_blocks, neighbours, send_rows, parent, slot):
    a_t = jnp.transpose(a_blocks, (1, 2, 3, 0)).reshape(4, 4096, E)
    r_t = jnp.transpose(r_blocks, (1, 2, 0)).reshape(4096, E)
    p_t = jnp.transpose(p_blocks, (1, 2, 0))
    me = lax.axis_index("grp").astype(jnp.int32).reshape(1)
    with jax.named_scope("exchange"):
        outgoing = send_blocks(jnp.transpose(send_rows, (2, 0, 1)), p_t.reshape(2, 32, 64, E))
        incoming = lax.all_to_all(outgoing.reshape(64, 96, 128), "dev", 0, 0, tiled=True).reshape(FAR, 32, 128)
    with jax.named_scope("near"):
        pairs, near, early_low, early_high, plan = near_terms(
            me, neighbours.T, slot.T, parent.reshape(1, E), a_t, r_t, p_t.reshape(4096, E)
        )

    def to_next(x):
        return lax.ppermute(x, "grp", [(i, (i + 1) % 4) for i in range(4)])

    def to_last(x):
        return lax.ppermute(x, "grp", [(i, (i + 3) % 4) for i in range(4)])

    with jax.named_scope("early"):
        early_low, early_high = to_next(early_low), to_last(early_high)
    with jax.named_scope("far"):
        far_low, far_high = far_terms((0,), ((BF16, BF16),), plan, incoming, pairs, near, "far_two")
        passed_low, passed_high = to_next(far_low), to_last(far_high)
        next_low, next_high, last_low, last_high = far_terms(
            (1, 2), ((F32, BF16), (BF16, F32)), plan, incoming, pairs, near, "far_one"
        )
        from_last_high, from_next_low = to_next(next_high), to_last(last_low)
        low, low_rest, high, high_rest = add_passed(
            next_low, early_low, passed_low, last_high, early_high, passed_high
        )
        from_last_low, from_next_high = to_next(low), to_last(high)
        low_rest, high_rest = to_next(low_rest), to_last(high_rest)
        (own,) = far_terms((3,), ((F32,),), plan, incoming, pairs, near, "far_own")
    with jax.named_scope("finish"):
        coarse = finish(0, FIRST, own, from_next_low, from_last_low, from_last_high, from_next_high)
        coarse = finish(FIRST, HALF - FIRST, own, from_next_low, low_rest, from_last_high, high_rest, coarse)
    return coarse.reshape(ROWS, SLOTS, 64, 64)


def solution(mesh):
    return jax.shard_map(
        on_device,
        mesh=mesh,
        in_specs=(
            P(("grp", "dev"), None, None, None),
            P(("grp", "dev"), None, None),
            P(("grp", "dev"), None, None),
            P(("grp", "dev"), None),
            P(("grp", "dev"), None, None),
            P(("grp", "dev")),
            P(("grp", "dev"), None),
        ),
        out_specs=P(("grp", "dev"), None, None, None),
        check_vma=False,
    )
```

```python
import functools

import jax
import jax.numpy as jnp
from jax import lax
from jax.experimental import pallas as pl
from jax.experimental.pallas import tpu as pltpu
from jax.sharding import PartitionSpec as P

MB = 1 << 20
F32 = jnp.float32
BF16 = jnp.bfloat16
VM = pltpu.VMEM
SM = pltpu.SMEM
HBM = pltpu.HBM

E = 128
SPAN = 32
ROWS = 16
SLOTS = 7
BLOCKS = ROWS * SLOTS
HALF = BLOCKS // 2
FAR = 192
CAP = 128
GROUP = 32
FAR_GROUP = 64
GROUPS = CAP // FAR_GROUP
CHUNKS = 4
SURE = 1
FIRST = 44
AREA = CAP
SUMS = 4 * AREA
COUNTS = 8 * AREA
PLAN = COUNTS + 1024
NEAR_AREA = 4 * SPAN + GROUP
ROOM = 3 * MB
AHEAD = (2, 1, 3, 0)


def rows_at(index, size):
    return pl.ds(pl.multiple_of(index * size, size), size)


def transpose_slabs(slab_of, steps, stride, wide, first=0):
    @pl.loop(0, steps, unroll=8)
    def _(i):
        wide[pl.ds(first + i, E, stride=stride), :] = slab_of(i).astype(F32).T


def send_kernel(rows, p_ref, out_ref, rows_here, blocks, wide, outgoing, arrived, written):
    rows_copy = pltpu.make_async_copy(rows, rows_here, arrived.at[4])
    rows_copy.start()
    copies = [
        pltpu.make_async_copy(p_ref.at[:, pl.ds(c * 8, 8)], blocks.at[c], arrived.at[c]) for c in range(4)
    ]
    for copy in copies:
        copy.start()
    for c in range(4):
        copies[c].wait()
        transpose_slabs(lambda i: blocks[c, :, i].reshape(128, E), 8, 40, wide, c * 8)
    rows_copy.wait()

    copies = []
    for c in range(CHUNKS):
        size = FAR // CHUNKS

        @pl.loop(0, 64 // CHUNKS, unroll=4)
        def _(n):
            peer = c * (64 // CHUNKS) + n
            for s in range(3):
                row = pl.multiple_of(rows_here[s, 0, peer] * 40, 8)
                outgoing[peer * 3 + s] = wide[pl.ds(row, 32), :].astype(BF16)

        some = pl.ds(c * size, size)
        copies.append(pltpu.make_async_copy(outgoing.at[some], out_ref.at[some], written.at[c]))
        copies[-1].start()
    for copy in copies:
        copy.wait()


def send_blocks(rows, p_t):
    return pl.pallas_call(
        send_kernel,
        out_shape=jax.ShapeDtypeStruct((FAR, 32, 128), BF16),
        in_specs=[pl.BlockSpec(memory_space=HBM)] * 2,
        out_specs=pl.BlockSpec(memory_space=HBM),
        scratch_shapes=[
            SM((3, 1, 64), jnp.int32),
            VM((4, 2, 8, 64, E), BF16),
            VM((E * 40 + 40, 128), F32),
            VM((FAR, 32, 128), BF16),
            pltpu.SemaphoreType.DMA((5,)),
            pltpu.SemaphoreType.DMA((CHUNKS,)),
        ],
        compiler_params=pltpu.CompilerParams(vmem_limit_bytes=63 * MB),
        name="send_blocks",
    )(rows, p_t)


def term_of(pair, doubled):
    applied = jnp.dot(pair[:, :64], doubled, preferred_element_type=F32).astype(BF16)
    term = jnp.dot(pair[:, 64:], applied, preferred_element_type=F32)
    low = lax.broadcasted_iota(jnp.int32, (32, 128), 1) < 64
    return jnp.where(low, term[:32], term[32:])


def near_kernel(me, neighbours, slot, parent, a_in, r_in, p_in, *refs):
    far_pairs_out, sums_out, early_low, early_high, plan_out, a_ref, r_ref, p_ref, pairs, doubled = refs[:10]
    wide, far_pairs, sums, early, plan, near_pairs, near_blocks, near_sums, far_list, arrived, written = refs[10:]
    incoming = [pltpu.make_async_copy(p_in, p_ref, arrived.at[5]), pltpu.make_async_copy(r_in, r_ref, arrived.at[4])]
    incoming += [pltpu.make_async_copy(a_in.at[k], a_ref.at[k], arrived.at[k]) for k in range(4)]
    for copy in incoming:
        copy.start()
    copies = []

    near_counts, far_counts = [], []
    for part, ahead in enumerate(AHEAD):
        first = lax.rem(me[0] + ahead, 4) * SPAN

        def element(i, carry):
            near, far = carry
            e = first + i
            base = lax.rem(parent[0, e], ROWS) * SLOTS
            near_pairs[near] = e
            near_blocks[near] = e
            near_sums[near] = base + slot[0, e]
            near = near + 1
            for k in range(1, 4):
                code = neighbours[k - 1, e]
                block_sum = base + slot[k, e]
                near_pairs[near] = k * E + e
                near_blocks[near] = code
                near_sums[near] = block_sum
                far_list[far] = k * E + e
                plan[far] = code - E
                plan[SUMS + far] = block_sum
                here = (code < E).astype(jnp.int32)
                near = near + here
                far = far + (1 - here)
            return near, far

        near, far = lax.fori_loop(0, SPAN, element, (part * NEAR_AREA, part * AREA), unroll=2)
        near_counts.append(near - part * NEAR_AREA)
        far_counts.append(far - part * AREA)
        plan[COUNTS + part] = far_counts[-1]

        def pad_far(i, carry):
            plan[part * AREA + i] = 0
            plan[SUMS + part * AREA + i] = 0
            return carry

        lax.fori_loop(far_counts[-1], (far_counts[-1] + FAR_GROUP - 1) // FAR_GROUP * FAR_GROUP, pad_far, 0)

        def pad_near(i, carry):
            near_pairs[part * NEAR_AREA + i] = 4 * E
            near_blocks[part * NEAR_AREA + i] = 0
            near_sums[part * NEAR_AREA + i] = 0
            return carry

        lax.fori_loop(near_counts[-1], (near_counts[-1] + GROUP - 1) // GROUP * GROUP, pad_near, 0)

    copies.append(pltpu.make_async_copy(plan, plan_out.at[pl.ds(0, PLAN)], written.at[8]))
    copies[-1].start()

    def two(i):
        block = p_ref[rows_at(i, 64), :]
        return jnp.concatenate([block, block], 0)

    incoming[0].wait()
    transpose_slabs(two, 64, 72, wide)
    doubled[...] = wide[: E * 72].reshape(E, 72, 128)[:, :64].astype(BF16)
    incoming[1].wait()
    for k in range(4):
        incoming[2 + k].wait()
        transpose_slabs(
            lambda i: jnp.concatenate([a_ref[k, rows_at(i, 64), :], r_ref[rows_at(i, 64), :]], 0), 64, 72, wide
        )
        pairs[rows_at(k, E)] = wide[: E * 72].reshape(E, 72, 128)[:, :64].astype(BF16)
    pairs[4 * E] = jnp.zeros((64, 128), BF16)

    for part in range(4):
        start, many = part * AREA, far_counts[part]

        def keep(i, carry):
            far_pairs[part, i] = pairs[far_list[start + i]]
            return carry

        lax.fori_loop(0, many, keep, 0)

        def clear(i, carry):
            far_pairs[part, i] = jnp.zeros((64, 128), BF16)
            return carry

        lax.fori_loop(many, (many + FAR_GROUP - 1) // FAR_GROUP * FAR_GROUP, clear, 0)
        copies.append(pltpu.make_async_copy(far_pairs.at[part], far_pairs_out.at[part], written.at[part]))
        copies[-1].start()
        sums[part] = jnp.zeros((BLOCKS, 32, 128), F32)

        def group(g, carry):
            at = part * NEAR_AREA + g * GROUP
            found = [term_of(pairs[near_pairs[at + u]], doubled[near_blocks[at + u]]) for u in range(GROUP)]
            for u in range(GROUP):
                sums[part, near_sums[at + u]] += found[u]
            return carry

        lax.fori_loop(0, (near_counts[part] + GROUP - 1) // GROUP, group, 0)
        if part == 0:
            early[...] = sums[0].astype(BF16)
            for h, out in enumerate((early_low, early_high)):
                copies.append(pltpu.make_async_copy(early.at[pl.ds(h * HALF, HALF)], out, written.at[9 + h]))
                copies[-1].start()
        else:
            copies.append(pltpu.make_async_copy(sums.at[part], sums_out.at[part], written.at[4 + part]))
            copies[-1].start()

    for copy in copies:
        copy.wait()


def near_terms(me, neighbours, slot, parent, a_t, r_t, p_t):
    return pl.pallas_call(
        near_kernel,
        out_shape=[
            jax.ShapeDtypeStruct((4, CAP, 64, 128), BF16),
            jax.ShapeDtypeStruct((4, BLOCKS, 32, 128), F32),
            jax.ShapeDtypeStruct((HALF, 32, 128), BF16),
            jax.ShapeDtypeStruct((HALF, 32, 128), BF16),
        ]
        + [jax.ShapeDtypeStruct((ROOM,), jnp.int32)],
        in_specs=[pl.BlockSpec(memory_space=SM)] * 4 + [pl.BlockSpec(memory_space=HBM)] * 3,
        out_specs=[pl.BlockSpec(memory_space=HBM)] * 5,
        scratch_shapes=[
            VM((4, 4096, E), BF16),
            VM((4096, E), BF16),
            VM((4096, E), BF16),
            VM((4 * E + 1, 64, 128), BF16),
            VM((E, 64, 128), BF16),
            VM((E * 72 + 72, 128), F32),
            VM((4, CAP, 64, 128), BF16),
            VM((4, BLOCKS, 32, 128), F32),
            VM((BLOCKS, 32, 128), BF16),
            SM((PLAN,), jnp.int32),
            SM((4 * NEAR_AREA,), jnp.int32),
            SM((4 * NEAR_AREA,), jnp.int32),
            SM((4 * NEAR_AREA,), jnp.int32),
            SM((4 * AREA,), jnp.int32),
            pltpu.SemaphoreType.DMA((6,)),
            pltpu.SemaphoreType.DMA((11,)),
        ],
        compiler_params=pltpu.CompilerParams(vmem_limit_bytes=55 * MB),
        cost_estimate=pl.CostEstimate(flops=700_000_000, bytes_accessed=40_000_000, transcendentals=0),
        name="near_terms",
    )(me, neighbours, slot, parent, a_t, r_t, p_t)


def far_kernel(parts, kinds, plan_in, incoming, *refs):
    pairs_in, near_in, *outs = refs[:-6]
    plan, pairs, near, sums, arrived, plan_arrived = refs[-6:]
    plan_copy = pltpu.make_async_copy(plan_in.at[pl.ds(0, PLAN)], plan, plan_arrived)
    plan_copy.start()
    low = lax.broadcasted_iota(jnp.int32, (32, 128), 1) < 64

    def pairs_copy(n, g):
        some = pl.ds(g * FAR_GROUP, FAR_GROUP)
        return pltpu.make_async_copy(pairs_in.at[parts[n], some], pairs.at[n, some], arrived.at[n, g])

    def near_copy(n):
        return pltpu.make_async_copy(near_in.at[parts[n]], near.at[n], arrived.at[n, GROUPS])

    def doubled(block):
        x = incoming[block]
        turned = jnp.concatenate([x[:, 64:], x[:, :64]], 1)
        return jnp.concatenate([jnp.where(low, x, turned), jnp.where(low, turned, x)], 0)

    for n in range(len(parts)):
        for g in range(SURE):
            pairs_copy(n, g).start()
        if parts[n]:
            near_copy(n).start()
    plan_copy.wait()
    for n, part in enumerate(parts):
        for g in range(SURE, GROUPS):

            @pl.when(plan[COUNTS + part] > g * FAR_GROUP)
            def _(n=n, g=g):
                pairs_copy(n, g).start()


    for n, part in enumerate(parts):
        sums[...] = jnp.zeros_like(sums)
        start = part * AREA
        groups = (plan[COUNTS + part] + FAR_GROUP - 1) // FAR_GROUP

        def group(g, carry):
            at = g * FAR_GROUP
            pairs_copy(n, g).wait()
            found = [term_of(pairs[n, at + u], doubled(plan[start + at + u])) for u in range(FAR_GROUP)]
            for u in range(FAR_GROUP):
                sums[plan[SUMS + start + at + u]] += found[u]
            return carry

        lax.fori_loop(0, groups, group, 0)

        for g in range(SURE):

            @pl.when(groups <= g)
            def _(n=n, g=g):
                pairs_copy(n, g).wait()

        if part:
            near_copy(n).wait()
        size = BLOCKS // len(kinds[n])
        for h, kind in enumerate(kinds[n]):
            some = pl.ds(h * size, size)
            total = near[n, some] + sums[some] if part else sums[some]
            outs[2 * n + h][...] = total.astype(kind)


def far_terms(parts, kinds, plan, incoming, pairs, near, name):
    shapes = [(BLOCKS // len(some), kind) for some in kinds for kind in some]
    return pl.pallas_call(
        functools.partial(far_kernel, parts, kinds),
        in_specs=[pl.BlockSpec(memory_space=HBM), pl.BlockSpec(memory_space=VM)]
        + [pl.BlockSpec(memory_space=HBM)] * 2,
        out_specs=[pl.BlockSpec(memory_space=VM)] * len(shapes),
        scratch_shapes=[
            SM((PLAN,), jnp.int32),
            VM((len(parts), CAP, 64, 128), BF16),
            VM((len(parts), BLOCKS, 32, 128), F32),
            VM((BLOCKS, 32, 128), F32),
            pltpu.SemaphoreType.DMA((len(parts), GROUPS + 1)),
            pltpu.SemaphoreType.DMA,
        ],
        out_shape=[jax.ShapeDtypeStruct((size, 32, 128), kind) for size, kind in shapes],
        compiler_params=pltpu.CompilerParams(vmem_limit_bytes=48 * MB),
        cost_estimate=pl.CostEstimate(flops=100_000_000, bytes_accessed=6_000_000, transcendentals=0),
        name=name,
    )(plan, incoming, pairs, near)


def add_kernel(here_a, early_a, passed_a, here_b, early_b, passed_b, *outs):
    sides = (here_a, early_a, passed_a), (here_b, early_b, passed_b)
    for n, (here, early, passed) in enumerate(sides):
        total = (here[...] + early[...].astype(F32) + passed[...].astype(F32)).astype(BF16)
        outs[2 * n][...] = total[:FIRST]
        outs[2 * n + 1][...] = total[FIRST:]


def add_passed(*parts):
    return pl.pallas_call(
        add_kernel,
        out_shape=[jax.ShapeDtypeStruct((size, 32, 128), BF16) for size in (FIRST, HALF - FIRST)] * 2,
        in_specs=[pl.BlockSpec(memory_space=VM)] * 6,
        out_specs=[pl.BlockSpec(memory_space=VM)] * 4,
        compiler_params=pltpu.CompilerParams(vmem_limit_bytes=16 * MB),
        name="add_passed",
    )(*parts)


def finish_kernel(first, size, own, low_a, low_b, high_a, high_b, *refs):
    out_ref, totals, written = refs[-3:]
    copies = []
    step = size // 2
    for h, (one, other) in enumerate(((low_a, low_b), (high_a, high_b))):
        for c in range(2):
            at = first + c * step
            some = pl.ds(h * HALF + at, step)
            mine = pl.ds(h * size + c * step, step)
            total = own[some] + one[pl.ds(at, step)].astype(F32) + other[pl.ds(c * step, step)].astype(F32)
            totals[mine, :32] = total[:, :, :64]
            totals[mine, 32:] = total[:, :, 64:]
            copies.append(pltpu.make_async_copy(totals.at[mine], out_ref.at[some], written.at[2 * h + c]))
            copies[-1].start()
    for copy in copies:
        copy.wait()


def finish(first, size, *parts):
    return pl.pallas_call(
        functools.partial(finish_kernel, first, size),
        out_shape=jax.ShapeDtypeStruct((BLOCKS, 64, 64), F32),
        in_specs=[pl.BlockSpec(memory_space=VM)] * 5 + [pl.BlockSpec(memory_space=HBM)] * (len(parts) - 5),
        out_specs=pl.BlockSpec(memory_space=HBM),
        input_output_aliases={5: 0} if first else {},
        scratch_shapes=[VM((2 * size, 64, 64), F32), pltpu.SemaphoreType.DMA((4,))],
        compiler_params=pltpu.CompilerParams(vmem_limit_bytes=24 * MB),
        name=f"finish_{first}",
    )(*parts)


def on_device(a_blocks, r_blocks, p_blocks, neighbours, send_rows, parent, slot):
    a_t = jnp.transpose(a_blocks, (1, 2, 3, 0)).reshape(4, 4096, E)
    r_t = jnp.transpose(r_blocks, (1, 2, 0)).reshape(4096, E)
    p_t = jnp.transpose(p_blocks, (1, 2, 0))
    me = lax.axis_index("grp").astype(jnp.int32).reshape(1)
    with jax.named_scope("exchange"):
        outgoing = send_blocks(jnp.transpose(send_rows, (2, 0, 1)), p_t.reshape(2, 32, 64, E))
        incoming = lax.all_to_all(outgoing.reshape(64, 96, 128), "dev", 0, 0, tiled=True).reshape(FAR, 32, 128)
    with jax.named_scope("near"):
        pairs, near, early_low, early_high, plan = near_terms(
            me, neighbours.T, slot.T, parent.reshape(1, E), a_t, r_t, p_t.reshape(4096, E)
        )

    def to_next(x):
        return lax.ppermute(x, "grp", [(i, (i + 1) % 4) for i in range(4)])

    def to_last(x):
        return lax.ppermute(x, "grp", [(i, (i + 3) % 4) for i in range(4)])

    with jax.named_scope("early"):
        early_low, early_high = to_next(early_low), to_last(early_high)
    with jax.named_scope("far"):
        far_low, far_high = far_terms((0,), ((BF16, BF16),), plan, incoming, pairs, near, "far_two")
        passed_low, passed_high = to_next(far_low), to_last(far_high)
        next_low, next_high, last_low, last_high = far_terms(
            (1, 2), ((F32, BF16), (BF16, F32)), plan, incoming, pairs, near, "far_one"
        )
        from_last_high, from_next_low = to_next(next_high), to_last(last_low)
        low, low_rest, high, high_rest = add_passed(
            next_low, early_low, passed_low, last_high, early_high, passed_high
        )
        from_last_low, from_next_high = to_next(low), to_last(high)
        low_rest, high_rest = to_next(low_rest), to_last(high_rest)
        (own,) = far_terms((3,), ((F32,),), plan, incoming, pairs, near, "far_own")
    with jax.named_scope("finish"):
        coarse = finish(0, FIRST, own, from_next_low, from_last_low, from_last_high, from_next_high)
        coarse = finish(FIRST, HALF - FIRST, own, from_next_low, low_rest, from_last_high, high_rest, coarse)
    return coarse.reshape(ROWS, SLOTS, 64, 64)


def solution(mesh):
    return jax.shard_map(
        on_device,
        mesh=mesh,
        in_specs=(
            P(("grp", "dev"), None, None, None),
            P(("grp", "dev"), None, None),
            P(("grp", "dev"), None, None),
            P(("grp", "dev"), None),
            P(("grp", "dev"), None, None),
            P(("grp", "dev")),
            P(("grp", "dev"), None),
        ),
        out_specs=P(("grp", "dev"), None, None, None),
        check_vma=False,
    )
```
